256 devices in a mesh: blk: 32 (over y_hi, z, core), uly: 8 (over x, y_lo).
Axes of the slice: x: 4, y: 4 (y_hi: 2, y_lo: 2; y = y_hi * 2 + y_lo), z: 8, core: 2. Of those that a mesh axis runs over, the one named last changes fastest.
Arguments:
- block_in: bfloat16 [2, 64, 64, 3072], P(None, 'blk', 'uly'), may hold values from -6 to 6
- mod_shift: float32 [3072], replicated, may hold values from -3 to 3
- mod_scale: float32 [3072], replicated, may hold values from -0.5 to 0.8
- mod_gate: float32 [3072], replicated, may hold values from -6 to 6
- qkv_weight: bfloat16 [3, 3072, 3072], P(None, None, 'uly'), may hold values from -0.09021098 to 0.09021098
- q_gain: float32 [128], replicated, may hold values from 1.3 to 6.5
- k_gain: float32 [128], replicated, may hold values from 1.3 to 6.5
- out_weight: bfloat16 [3072, 3072], P('uly'), may hold values from -0.109375 to 0.109375
- final_shift: float32 [3072], replicated, may hold values from -3 to 3
- final_scale: float32 [3072], replicated, may hold values from -0.5 to 0.8
- final_weight: bfloat16 [3072, 64], replicated, may hold values from -0.109375 to 0.109375
- final_bias: float32 [64], replicated, may hold values from -3 to 3
- conv_weight: bfloat16 [3, 3, 3, 16, 512], replicated, may hold values from -0.3125 to 0.3125
- conv_bias: float32 [512], replicated, may hold values from -3 to 3
Outputs:
- block_out: bfloat16 [2, 64, 64, 3072], P(None, 'blk', 'uly')
- conv_out: bfloat16 [2, 128, 128, 512], P(None, 'blk', 'uly')
The draws below stay inside these ranges and needn't reach their ends.
All inputs are finite; a program needn't handle non-finite values.
Results may differ from the reference program's by a relative error of at most 0.019.
Values may be sent and summed in bfloat16 or wider, within the bound.
No kernel may reach another device: no remote copies, remote signals or barrier semaphores. Data moves between devices by JAX's collectives and lax.ppermute only.
A program may use at most 192 MiB of HBM per device.

```python
import math
import jax
import jax.numpy as jnp
from jax import lax

H = 24
HD = 128
D = 3072
LC = 16
CO = 512
RT = 16
RH = 56
F = 2
HB = 2
WB = 8
HT = 64
WT = 64
N_BLK = 32
N_ULY = 8


def draw_qkv_weight(key, part):
    key = jax.random.fold_in(key, 17)
    spread = D ** (-0.5)
    base = jax.random.normal(key, (3, D, D), jnp.float32) * spread
    return jnp.clip(base, -4.95 * spread, 4.95 * spread).astype(jnp.bfloat16)


def gain_draw(key, lowest, highest):
    return jnp.exp(jax.random.uniform(key, (HD,), jnp.float32, math.log(lowest), math.log(highest)))


def draw_q_gain(key, part):
    key = jax.random.fold_in(key, 23)
    return gain_draw(key, 1.3, 2.6)


def draw_k_gain(key, part):
    key = jax.random.fold_in(key, 29)
    return gain_draw(key, 1.3, 2.6)


def level_of(rng, dims, shards, smallest, top_value):
    level, own = 1.0, jax.random.fold_in(rng, 6)
    for dim, parts in shards:
        draws = jnp.exp(jax.random.uniform(jax.random.fold_in(own, dim), (parts,), jnp.float32, smallest / len(shards), top_value / len(shards)))
        level = level * jnp.repeat(draws, dims[dim] // parts).reshape([-1 if axis == dim else 1 for axis in range(len(dims))])
    return level


def normal_values(key, extent, scale, limit, shards=(), held_as=jnp.bfloat16):
    entries = scale * jax.random.normal(key, extent, jnp.float32)
    if shards:
        entries = entries * level_of(key, extent, shards, -0.22, 0.18)
    return jnp.clip(entries, -limit, limit).astype(held_as)


def setup_inputs(seed: int = 0) -> dict:
    seeds = jax.random.split(jax.random.key(seed), 15)
    block_in = normal_values(seeds[0], (F, HT, WT, D), 1.0, 6.0, ((1, 32), (2, 8)))
    mod_shift = normal_values(seeds[1], (D,), 0.5, 3.0, (), jnp.float32)
    mod_scale = jnp.clip(jax.random.uniform(seeds[2], (D,), jnp.float32, -0.5, 0.8), -0.5, 0.8)
    mod_gate = normal_values(seeds[3], (D,), 1.5, 6.0, (), jnp.float32)
    qkv_weight = draw_qkv_weight(jax.random.fold_in(seeds[14], 71), 0)
    q_gain = draw_q_gain(jax.random.fold_in(seeds[14], 71), 0)
    k_gain = draw_k_gain(jax.random.fold_in(seeds[14], 71), 0)
    out_weight = normal_values(seeds[7], (D, D), D ** -0.5, 0.109375, ((0, 8),))
    final_shift = normal_values(seeds[8], (D,), 0.5, 3.0, (), jnp.float32)
    final_scale = jnp.clip(jax.random.uniform(seeds[9], (D,), jnp.float32, -0.5, 0.8), -0.5, 0.8)
    final_weight = normal_values(seeds[10], (D, 4 * LC), D ** -0.5, 0.109375)
    final_bias = normal_values(seeds[11], (4 * LC,), 0.5, 3.0, (), jnp.float32)
    conv_weight = normal_values(seeds[12], (3, 3, 3, LC, CO), (27 * LC) ** -0.5, 0.3125)
    conv_bias = normal_values(seeds[13], (CO,), 0.5, 3.0, (), jnp.float32)
    return dict(block_in=block_in, mod_shift=mod_shift, mod_scale=mod_scale, mod_gate=mod_gate, qkv_weight=qkv_weight, q_gain=q_gain, k_gain=k_gain, out_weight=out_weight, final_shift=final_shift, final_scale=final_scale, final_weight=final_weight, final_bias=final_bias, conv_weight=conv_weight, conv_bias=conv_bias)


def layer_norm(values):
    center = values - lax.optimization_barrier(jnp.mean(values, axis=-1, keepdims=True))
    spread = lax.optimization_barrier(jnp.mean(center * center, axis=-1, keepdims=True))
    return center * lax.rsqrt(spread + 1e-06)

def head_norm(values, gain):
    return values * lax.rsqrt(lax.optimization_barrier(jnp.mean(values * values, axis=-1, keepdims=True)) + 1e-06) * gain

def rotate(values, frames_at, rows_at, columns_at):
    pieces = []
    offset = 0
    for position, length in ((frames_at, RT), (rows_at, RH), (columns_at, RH)):
        half = length // 2
        rates = 256.0 ** (-2.0 * jnp.arange(half, dtype=jnp.float32) / length)
        angles = position[:, None] * rates[None, :]
        cosine = jnp.cos(angles)[:, None, :]
        sine_part = jnp.sin(angles)[:, None, :]
        lower = values[..., offset:offset + half]
        upper = values[..., offset + half:offset + length]
        pieces.append(lower * cosine - upper * sine_part)
        pieces.append(upper * cosine + lower * sine_part)
        offset += length
    return jnp.concatenate(pieces, axis=-1)

def reference(block_in, mod_shift, mod_scale, mod_gate, qkv_weight, q_gain, k_gain, out_weight, final_shift, final_scale, final_weight, final_bias, conv_weight, conv_bias):
    height = HB * N_BLK
    breadth = WB * N_ULY
    count = F * height * breadth
    tokens_in = block_in.reshape(count, D).astype(jnp.float32)
    x_mod = (layer_norm(tokens_in) * (1.0 + mod_scale) + mod_shift).astype(jnp.bfloat16)
    numbers = jnp.arange(count, dtype=jnp.int32)
    frames_at = (numbers // (height * breadth)).astype(jnp.float32)
    rows_at = (numbers // breadth % height).astype(jnp.float32)
    columns_at = (numbers % breadth).astype(jnp.float32)
    scale = HD ** (-0.5)

    def one_head(head):
        weights = lax.dynamic_slice_in_dim(qkv_weight, head * HD, HD, 2)
        raw_query = jnp.dot(x_mod, weights[0], preferred_element_type=jnp.float32)
        raw_key = jnp.dot(x_mod, weights[1], preferred_element_type=jnp.float32)
        values = jnp.dot(x_mod, weights[2], preferred_element_type=jnp.float32).astype(jnp.bfloat16)
        queries = rotate(head_norm(raw_query, q_gain)[:, None, :], frames_at, rows_at, columns_at)[:, 0, :].astype(jnp.bfloat16)
        keys = rotate(head_norm(raw_key, k_gain)[:, None, :], frames_at, rows_at, columns_at)[:, 0, :].astype(jnp.bfloat16)
        blocks = queries.reshape(N_BLK, count // N_BLK, HD)

        def attend(block):
            scores = jnp.dot(block, keys.T, preferred_element_type=jnp.float32) * scale
            raised = jnp.exp(scores - lax.optimization_barrier(jnp.max(scores, axis=-1, keepdims=True)))
            denominator = lax.optimization_barrier(jnp.sum(raised, axis=-1, keepdims=True))
            probs = raised.astype(jnp.bfloat16)
            return (jnp.dot(probs, values, preferred_element_type=jnp.float32) / denominator).astype(jnp.bfloat16)
        return lax.map(attend, blocks).reshape(count, HD)
    attended = lax.map(one_head, jnp.arange(H, dtype=jnp.int32))
    attended = jnp.transpose(attended, (1, 0, 2)).reshape(count, D)
    attn_proj = jnp.dot(attended, out_weight, preferred_element_type=jnp.float32)
    block_out = (tokens_in + mod_gate * attn_proj).astype(jnp.bfloat16)
    final_in = (layer_norm(block_out.astype(jnp.float32)) * (1.0 + final_scale) + final_shift).astype(jnp.bfloat16)
    latent_tok = (jnp.dot(final_in, final_weight, preferred_element_type=jnp.float32) + final_bias).astype(jnp.bfloat16)
    latent = latent_tok.reshape(F, height, breadth, LC, 2, 2).transpose(0, 1, 4, 2, 5, 3).reshape(F, 2 * height, 2 * breadth, LC)
    padded = jnp.pad(latent, ((2, 0), (1, 1), (1, 1), (0, 0)), mode='edge')
    total = jnp.zeros((F, 2 * height, 2 * breadth, CO), jnp.float32) + conv_bias
    for time_lag in range(3):
        for row_lag in range(3):
            for column_lag in range(3):
                window = padded[time_lag:time_lag + F, row_lag:row_lag + 2 * height, column_lag:column_lag + 2 * breadth]
                total = total + jnp.dot(window, conv_weight[time_lag, row_lag, column_lag], preferred_element_type=jnp.float32)
    return (block_out.reshape(F, height, breadth, D), total.astype(jnp.bfloat16))
```

```python
import functools

import jax
import jax.numpy as jnp
import numpy as np
from jax import lax
from jax.experimental import pallas as pl
from jax.experimental.pallas import tpu as pltpu
from jax.sharding import PartitionSpec as P

HD = 128
RT = 16
RH = 56
Z = 8
X = 4
HEADS = 3
GROUP = HEADS * HD
WIDTH = 3072
LOCAL = 32
PAIR = 2 * LOCAL
TOKENS = X * PAIR
STATS = 128
SCALE2 = float(HD ** (-0.5) / np.log(2.0))
F32 = jnp.float32
BF16 = jnp.bfloat16


def params(mib=40):
    return pltpu.CompilerParams(vmem_limit_bytes=mib * 1024 * 1024)


def full(shape):
    return pl.BlockSpec(shape, lambda *_: (0,) * len(shape))


def blk_pairs(dy, dz, dc):
    return [
        (y * 2 * Z + z * 2 + c, (y ^ dy) * 2 * Z + (z + dz) % Z * 2 + (c ^ dc))
        for y in range(2)
        for z in range(Z)
        for c in range(2)
    ]


def uly_pairs(dx, dy):
    return [(x * 2 + y, (x + dx) % X * 2 + (y ^ dy)) for x in range(X) for y in range(2)]


def send_blk(value, dy=0, dz=0, dc=0):
    return lax.ppermute(value, "blk", blk_pairs(dy, dz, dc))


def send_uly(value, dx=0, dy=0):
    return lax.ppermute(value, "uly", uly_pairs(dx, dy))


def normed(values):
    center = values - jnp.mean(values, axis=-1, keepdims=True)
    spread = jnp.mean(center * center, axis=-1, keepdims=True)
    return center * lax.rsqrt(spread + 1e-06)


def modulate_kernel(tokens, shift, scale, out):
    out[...] = (normed(tokens[...].astype(F32)) * (1.0 + scale[...]) + shift[...]).astype(BF16)


def modulate(tokens, shift, scale):
    return pl.pallas_call(
        modulate_kernel,
        out_shape=jax.ShapeDtypeStruct((LOCAL, WIDTH), BF16),
        compiler_params=params(),
    )(tokens, shift, scale)


def rope_tables():
    uly = lax.axis_index("uly")
    lane = np.arange(HD)
    section = np.where(lane < RT, 0, np.where(lane < RT + RH, 1, 2))
    start = np.array([0, RT, RT + RH])[section]
    length = np.array([RT, RH, RH])[section]
    half = length // 2
    upper = (lane - start) >= half
    index = jnp.asarray((lane - start) % half, F32)
    rates = 256.0 ** (-2.0 * index / jnp.asarray(length, F32))
    place = jnp.arange(TOKENS, dtype=jnp.int32)
    dx, dy, within = place // PAIR, place // LOCAL % 2, place % LOCAL
    member = (uly // 2 - dx) % X * 2 + (uly % 2 + dy) % 2
    frames_at = within // 16
    rows_at = lax.axis_index("blk") * 2 + within // 8 % 2
    columns_at = member * 8 + within % 8
    where = jnp.where(
        section[None, :] == 0,
        frames_at[:, None],
        jnp.where(section[None, :] == 1, rows_at[:, None], columns_at[:, None]),
    ).astype(F32)
    angles = where * rates[None, :]
    sign = jnp.asarray(np.where(upper, 1.0, -1.0), F32)
    return jnp.cos(angles), jnp.sin(angles) * sign[None, :]


def rope_partner(values):
    lane = lax.broadcasted_iota(jnp.int32, values.shape, 1)
    time_half, space_half = RT // 2, RH // 2
    first = jnp.where(
        lane < time_half,
        pltpu.roll(values, HD - time_half, axis=1),
        pltpu.roll(values, time_half, axis=1),
    )
    low = (lane < RT + space_half) | ((lane >= RT + RH) & (lane < RT + RH + space_half))
    rest = jnp.where(
        low, pltpu.roll(values, HD - space_half, axis=1), pltpu.roll(values, space_half, axis=1)
    )
    return jnp.where(lane < RT, first, rest)


def project_kernel(first_part, x0, x1, x2, x3, weight, gain, cosine, sine, out):
    part = pl.program_id(0) + first_part
    for piece, ref in enumerate((x0, x1, x2, x3)):
        rows = pl.ds(piece * PAIR, PAIR)
        mixed = jnp.dot(ref[...], weight[0], preferred_element_type=F32)

        @pl.when(part == 2)
        def _():
            out[0, rows, :] = mixed.astype(BF16)

        @pl.when(part < 2)
        def _():
            for head in range(HEADS):
                lanes = slice(head * HD, (head + 1) * HD)
                one = mixed[:, lanes]
                one = one * lax.rsqrt(jnp.mean(one * one, axis=-1, keepdims=True) + 1e-06)
                one = one * gain[0]
                turned = one * cosine[rows, :] + rope_partner(one) * sine[rows, :]
                out[0, rows, lanes] = turned.astype(BF16)


def project(first_part, parts, pieces, weight, gains, cosine, sine):
    return pl.pallas_call(
        functools.partial(project_kernel, first_part),
        grid=(parts,),
        in_specs=[full((PAIR, WIDTH))] * 4
        + [
            pl.BlockSpec((1, WIDTH, GROUP), lambda s: (s + first_part, 0, 0)),
            pl.BlockSpec((1, 1, HD), lambda s: (jnp.minimum(s + first_part, 1), 0, 0)),
            full((TOKENS, HD)),
            full((TOKENS, HD)),
        ],
        out_specs=pl.BlockSpec((1, TOKENS, GROUP), lambda s: (s, 0, 0)),
        out_shape=jax.ShapeDtypeStruct((parts, TOKENS, GROUP), BF16),
        compiler_params=params(),
    )(*pieces, weight, gains, cosine, sine)


def set_lane(values, lane, column):
    at = lax.broadcasted_iota(jnp.int32, values.shape, 1)
    return jnp.where(at == lane, column, values)


def attend_kernel(counts, fresh, last, *refs):
    refs = list(refs)
    queries = refs.pop(0)
    blocks = [refs.pop(0) for _ in counts]
    if not fresh:
        old_sum, old_stat = refs.pop(0), refs.pop(0)
    total = refs.pop(0)
    rows = queries.shape[0]
    if not last:
        stat = refs.pop(0)
    stats = jnp.zeros((rows, STATS), F32)
    for head in range(HEADS):
        lanes = slice(head * HD, (head + 1) * HD)
        query = queries[:, lanes]
        scores = [
            lax.dot_general(
                query, ref[0, :, lanes], (((1,), (1,)), ((), ())), preferred_element_type=F32
            )
            for ref in blocks
        ]
        top = functools.reduce(
            jnp.maximum, [jnp.max(score, axis=-1, keepdims=True) for score in scores]
        )
        if not fresh:
            old_top = old_stat[:, head : head + 1]
            top = jnp.maximum(top, old_top)
            fade = jnp.exp2((old_top - top) * SCALE2)
        shift = top * SCALE2
        sums = None
        for score, ref, count in zip(scores, blocks, counts):
            probs = jnp.exp2(score * SCALE2 - shift).astype(BF16)
            values = jnp.concatenate([ref[1, :, lanes], jnp.ones((count, HD), BF16)], axis=1)
            part = jnp.dot(probs, values, preferred_element_type=F32)
            sums = part if sums is None else sums + part
        numerator = sums[:, :HD]
        denominator = sums[:, HD : HD + 1]
        if not fresh:
            numerator = numerator + old_sum[:, lanes] * fade
            denominator = denominator + old_stat[:, HEADS + head : HEADS + head + 1] * fade
        if last:
            total[:, lanes] = (numerator / denominator).astype(BF16)
            level = shift + jnp.log2(denominator)
            for piece in range(3):
                coarse = level.astype(BF16).astype(F32)
                stats = set_lane(stats, head * 3 + piece, coarse)
                level = level - coarse
        else:
            total[:, lanes] = numerator
            stats = set_lane(stats, head, top)
            stats = set_lane(stats, HEADS + head, denominator)
    if last:
        total[:, GROUP:] = stats.astype(BF16)
    else:
        stat[...] = stats


def attend(queries, blocks, state, last):
    count = queries.shape[0]
    tile = TOKENS
    fresh = state is None
    by_rows = lambda width: pl.BlockSpec((tile, width), lambda i: (i, 0))
    if last:
        out_specs = by_rows(GROUP + STATS)
        out_shape = jax.ShapeDtypeStruct((count, GROUP + STATS), BF16)
    else:
        out_specs = [by_rows(GROUP), by_rows(STATS)]
        out_shape = [
            jax.ShapeDtypeStruct((count, GROUP), F32),
            jax.ShapeDtypeStruct((count, STATS), F32),
        ]
    return pl.pallas_call(
        functools.partial(attend_kernel, tuple(block.shape[1] for block in blocks), fresh, last),
        grid=(count // tile,),
        in_specs=[by_rows(GROUP)]
        + [full(block.shape) for block in blocks]
        + ([] if fresh else [by_rows(GROUP), by_rows(STATS)]),
        out_specs=out_specs,
        out_shape=out_shape,
        compiler_params=params(),
    )(queries, *blocks, *(() if fresh else state))


def merged(parts):
    tails = [part[:, GROUP:].astype(F32) for part in parts]
    outs, levels = [], []
    for head in range(HEADS):
        lanes = slice(head * HD, (head + 1) * HD)
        level = [
            tail[:, 3 * head : 3 * head + 1]
            + tail[:, 3 * head + 1 : 3 * head + 2]
            + tail[:, 3 * head + 2 : 3 * head + 3]
            for tail in tails
        ]
        top = functools.reduce(jnp.maximum, level)
        shares = [jnp.exp2(one - top) for one in level]
        whole = functools.reduce(jnp.add, shares)
        mixed = functools.reduce(
            jnp.add, [part[:, lanes].astype(F32) * share for part, share in zip(parts, shares)]
        )
        outs.append(mixed / whole)
        levels.append(top + jnp.log2(whole))
    return outs, levels


def merge_kernel(mine, theirs, out):
    outs, levels = merged([mine[...], theirs[...]])
    stats = jnp.zeros((mine.shape[0], STATS), F32)
    for head in range(HEADS):
        out[:, head * HD : (head + 1) * HD] = outs[head].astype(BF16)
        level = levels[head]
        for piece in range(3):
            coarse = level.astype(BF16).astype(F32)
            stats = set_lane(stats, head * 3 + piece, coarse)
            level = level - coarse
    out[:, GROUP:] = stats.astype(BF16)


def merge(mine, theirs):
    wide = GROUP + STATS
    return pl.pallas_call(
        merge_kernel,
        grid=(1,),
        in_specs=[pl.BlockSpec((TOKENS, wide), lambda i: (1, 0))] * 2,
        out_specs=pl.BlockSpec((TOKENS, wide), lambda i: (0, 0)),
        out_shape=jax.ShapeDtypeStruct((TOKENS, wide), BF16),
        compiler_params=params(),
    )(mine, theirs)


def out_kernel(mine, theirs, across, weight, *outs):
    heads, _ = merged([mine[...], theirs[...], across[...]])
    attended = jnp.concatenate([head.astype(BF16) for head in heads], axis=1)
    product = jnp.dot(attended, weight[...], preferred_element_type=F32)
    for piece, out in enumerate(outs):
        out[...] = product[piece * PAIR : (piece + 1) * PAIR].astype(BF16)


def out_project(mine, theirs, across, weight):
    wide = GROUP + STATS
    tile = 1024
    return pl.pallas_call(
        out_kernel,
        grid=(WIDTH // tile,),
        in_specs=[full((TOKENS, wide))] * 3 + [pl.BlockSpec((GROUP, tile), lambda i: (0, i))],
        out_specs=[pl.BlockSpec((PAIR, tile), lambda i: (0, i))] * X,
        out_shape=[jax.ShapeDtypeStruct((PAIR, WIDTH), BF16)] * X,
        compiler_params=params(),
    )(mine, theirs, across, weight)


def half_sum_kernel(a, b, c, d, keep, send):
    total = (a[...].astype(F32) + b[...].astype(F32)) + (c[...].astype(F32) + d[...].astype(F32))
    keep[...] = total[:LOCAL]
    send[...] = total[LOCAL:].astype(BF16)


def half_sum(parts):
    return pl.pallas_call(
        half_sum_kernel,
        out_shape=[
            jax.ShapeDtypeStruct((LOCAL, WIDTH), F32),
            jax.ShapeDtypeStruct((LOCAL, WIDTH), BF16),
        ],
        compiler_params=params(),
    )(*parts)


def final_kernel(tokens, keep, came, gate, shift, scale, weight, bias, block_out, latent):
    projected = keep[...] + came[...].astype(F32)
    result = (tokens[...].astype(F32) + gate[...] * projected).astype(BF16)
    block_out[...] = result
    final_in = (normed(result.astype(F32)) * (1.0 + scale[...]) + shift[...]).astype(BF16)
    mixed = jnp.dot(final_in, weight[...], preferred_element_type=F32)
    latent[...] = (mixed + bias[...]).astype(BF16)


def final(tokens, keep, came, gate, shift, scale, weight, bias):
    return pl.pallas_call(
        final_kernel,
        out_shape=[
            jax.ShapeDtypeStruct((LOCAL, WIDTH), BF16),
            jax.ShapeDtypeStruct((LOCAL, bias.shape[1]), BF16),
        ],
        compiler_params=params(),
    )(tokens, keep, came, gate, shift, scale, weight, bias)


def extended(block, sides, width):
    for axis, dim in sides:
        count = lax.axis_size(axis)
        place = lax.axis_index(axis)
        forward = [(i, i + 1) for i in range(count - 1)]
        backward = [(target, source) for source, target in forward]
        first = lax.slice_in_dim(block, 0, width, axis=dim)
        end = lax.slice_in_dim(block, block.shape[dim] - width, None, axis=dim)
        low = jnp.where(place == 0, first, lax.ppermute(end, axis, forward))
        high = jnp.where(place == count - 1, end, lax.ppermute(first, axis, backward))
        block = jnp.concatenate([low, block, high], axis=dim)
    return block


def local(
    block_in,
    mod_shift,
    mod_scale,
    mod_gate,
    qkv_weight,
    q_gain,
    k_gain,
    out_weight,
    final_shift,
    final_scale,
    final_weight,
    final_bias,
    conv_weight,
    conv_bias,
):
    frames, rows, columns, width = block_in.shape
    tokens = block_in.reshape(LOCAL, WIDTH)
    row = lambda vector: vector.reshape(1, -1)
    x_mod = modulate(tokens, row(mod_shift), row(mod_scale))
    pair = jnp.concatenate([x_mod, send_uly(x_mod, dy=1)], axis=0)
    pieces = [pair] + [send_uly(pair, dx=step) for step in range(1, X)]
    cosine, sine = rope_tables()
    gains = jnp.stack([q_gain, k_gain]).reshape(2, 1, HD)

    key_value = project(1, 2, pieces, qkv_weight, gains, cosine, sine)
    query = project(0, 1, pieces, qkv_weight, gains, cosine, sine).reshape(TOKENS, GROUP)
    queries = jnp.concatenate([query, send_blk(query, dc=1)], axis=0)
    near, far = queries, send_blk(queries, dy=1)
    queries = jnp.concatenate(
        [near[:TOKENS], far[:TOKENS], near[TOKENS:], far[TOKENS:]], axis=0
    )

    low = high = key_value
    state = None
    waiting = [key_value]
    for _ in range(Z // 2 - 1):
        low, high = send_blk(low, dz=1), send_blk(high, dz=-1)
        state = attend(queries, waiting + [low, high], state, False)
        waiting = []
    middle = TOKENS // 2
    ends = [send_blk(low[:, :middle], dz=1), send_blk(high[:, middle:], dz=-1)]
    partial = attend(queries, ends, state, True)

    mine = partial[: 2 * TOKENS]
    theirs = send_blk(partial[2 * TOKENS :], dc=1)
    across = send_blk(merge(mine, theirs), dy=1)
    shares = out_project(mine, theirs, across, out_weight)
    arrived = [shares[0]] + [send_uly(shares[step], dx=-step) for step in range(1, X)]
    keep, leave = half_sum(arrived)
    block_out, latent_tok = final(
        tokens,
        keep,
        send_uly(leave, dy=1),
        row(mod_gate),
        row(final_shift),
        row(final_scale),
        final_weight,
        row(final_bias),
    )

    channels = final_bias.shape[0] // 4
    latent = (
        latent_tok.reshape(frames, rows, columns, channels, 2, 2)
        .transpose(0, 1, 4, 2, 5, 3)
        .reshape(frames, 2 * rows, 2 * columns, channels)
    )
    padded = extended(latent, (("blk", 1), ("uly", 2)), 1)
    padded = jnp.concatenate([padded[:1], padded[:1], padded], axis=0)
    windows = []
    for time_lag in range(3):
        for row_lag in range(3):
            for column_lag in range(3):
                windows.append(
                    padded[
                        time_lag : time_lag + frames,
                        row_lag : row_lag + 2 * rows,
                        column_lag : column_lag + 2 * columns,
                    ]
                )
    patches = jnp.concatenate(windows, axis=-1)
    kernel = conv_weight.reshape(27 * channels, conv_weight.shape[-1])
    conv_out = (jnp.dot(patches, kernel, preferred_element_type=F32) + conv_bias).astype(BF16)
    return (block_out.reshape(frames, rows, columns, width), conv_out)


def solution(mesh):
    in_specs = (
        P(None, "blk", "uly", None),
        P(),
        P(),
        P(),
        P(None, None, "uly"),
        P(),
        P(),
        P("uly", None),
        P(),
        P(),
        P(),
        P(),
        P(),
        P(),
    )
    out_specs = (P(None, "blk", "uly", None), P(None, "blk", "uly", None))
    return jax.shard_map(local, mesh=mesh, in_specs=in_specs, out_specs=out_specs, check_vma=False)
```

```python
import functools

import jax
import jax.numpy as jnp
import numpy as np
from jax import lax
from jax.experimental import pallas as pl
from jax.experimental.pallas import tpu as pltpu
from jax.sharding import PartitionSpec as P

HD = 128
RT = 16
RH = 56
Z = 8
X = 4
HEADS = 3
GROUP = HEADS * HD
WIDTH = 3072
LOCAL = 32
PAIR = 2 * LOCAL
TOKENS = X * PAIR
STATS = 16
HALF = WIDTH // 2
SCALE2 = float(HD ** (-0.5) / np.log(2.0))
F32 = jnp.float32
BF16 = jnp.bfloat16


def params(mib=32):
    return pltpu.CompilerParams(vmem_limit_bytes=mib * 1024 * 1024)


def whole():
    return pl.BlockSpec(memory_space=pltpu.VMEM)


def full(shape):
    return pl.BlockSpec(shape, lambda *_: (0,) * len(shape))


def blk_pairs(dy, dz, dc):
    return [
        (y * 2 * Z + z * 2 + c, (y ^ dy) * 2 * Z + (z + dz) % Z * 2 + (c ^ dc))
        for y in range(2)
        for z in range(Z)
        for c in range(2)
    ]


def uly_pairs(dx, dy):
    return [(x * 2 + y, (x + dx) % X * 2 + (y ^ dy)) for x in range(X) for y in range(2)]


def send_blk(value, dy=0, dz=0, dc=0):
    return lax.ppermute(value, "blk", blk_pairs(dy, dz, dc))


def send_uly(value, dx=0, dy=0):
    return lax.ppermute(value, "uly", uly_pairs(dx, dy))


def normed(values):
    center = values - jnp.mean(values, axis=-1, keepdims=True)
    spread = jnp.mean(center * center, axis=-1, keepdims=True)
    return center * lax.rsqrt(spread + 1e-06)


def modulate_kernel(tokens, shift, scale, *halves):
    x_mod = (normed(tokens[...].astype(F32)) * (1.0 + scale[...]) + shift[...]).astype(BF16)
    halves[0][...] = x_mod[:, :HALF]
    halves[1][...] = x_mod[:, HALF:]


def modulate(tokens, shift, scale):
    return pl.pallas_call(
        modulate_kernel,
        grid=(1,),
        in_specs=[full((LOCAL, WIDTH)), full((1, WIDTH)), full((1, WIDTH))],
        out_specs=[full((LOCAL, HALF))] * 2,
        out_shape=[jax.ShapeDtypeStruct((LOCAL, HALF), BF16)] * 2,
        compiler_params=params(),
    )(tokens, shift, scale)


def fetch_kernel(weight, after, out, sem):
    copy = pltpu.make_async_copy(weight, out, sem)
    copy.start()
    copy.wait()


def fetch(weight, after):
    return pl.pallas_call(
        fetch_kernel,
        in_specs=[pl.BlockSpec(memory_space=pl.ANY)] * 2,
        out_specs=whole(),
        out_shape=jax.ShapeDtypeStruct(weight.shape, weight.dtype),
        scratch_shapes=[pltpu.SemaphoreType.DMA],
        compiler_params=params(),
    )(weight, after)


def rope_tables():
    uly = lax.axis_index("uly")
    lane = np.arange(HD)
    section = np.where(lane < RT, 0, np.where(lane < RT + RH, 1, 2))
    start = np.array([0, RT, RT + RH])[section]
    length = np.array([RT, RH, RH])[section]
    half = length // 2
    upper = (lane - start) >= half
    index = jnp.asarray((lane - start) % half, F32)
    rates = 256.0 ** (-2.0 * index / jnp.asarray(length, F32))
    place = jnp.arange(TOKENS, dtype=jnp.int32)
    dx, dy, within = place // PAIR, place // LOCAL % 2, place % LOCAL
    member = (uly // 2 - dx) % X * 2 + (uly % 2 + dy) % 2
    frames_at = within // 16
    rows_at = lax.axis_index("blk") * 2 + within // 8 % 2
    columns_at = member * 8 + within % 8
    where = jnp.where(
        section[None, :] == 0,
        frames_at[:, None],
        jnp.where(section[None, :] == 1, rows_at[:, None], columns_at[:, None]),
    ).astype(F32)
    angles = where * rates[None, :]
    sign = jnp.asarray(np.where(upper, 1.0, -1.0), F32)
    return jnp.cos(angles), jnp.sin(angles) * sign[None, :]


def rope_partner(values):
    lane = lax.broadcasted_iota(jnp.int32, values.shape, 1)
    time_half, space_half = RT // 2, RH // 2
    first = jnp.where(
        lane < time_half,
        pltpu.roll(values, HD - time_half, axis=1),
        pltpu.roll(values, time_half, axis=1),
    )
    low = (lane < RT + space_half) | ((lane >= RT + RH) & (lane < RT + RH + space_half))
    rest = jnp.where(
        low, pltpu.roll(values, HD - space_half, axis=1), pltpu.roll(values, space_half, axis=1)
    )
    return jnp.where(lane < RT, first, rest)


def headed(mixed, gain, cosine, sine):
    out = []
    for head in range(HEADS):
        one = mixed[:, head * HD : (head + 1) * HD]
        one = one * lax.rsqrt(jnp.mean(one * one, axis=-1, keepdims=True) + 1e-06) * gain
        out.append((one * cosine + rope_partner(one) * sine).astype(BF16))
    return jnp.concatenate(out, axis=1)


def key_value_kernel(a0, a1, a2, a3, b0, b1, weight, gain, cosine, sine, out, gathered):
    for step, ref in enumerate((a0, a1, a2, a3)):
        gathered[step * PAIR : (step + 1) * PAIR, :HALF] = ref[...]
        for side, other in enumerate((b0, b1)):
            start = step * PAIR + side * LOCAL
            gathered[start : start + LOCAL, HALF:] = other[step * LOCAL : (step + 1) * LOCAL, :]
    keys = jnp.dot(gathered[...], weight[1], preferred_element_type=F32)
    out[0] = headed(keys, gain[...], cosine[...], sine[...])
    out[1] = jnp.dot(gathered[...], weight[2], preferred_element_type=F32).astype(BF16)


def project_key_value(pieces, weight, gain, cosine, sine):
    return pl.pallas_call(
        key_value_kernel,
        out_shape=[
            jax.ShapeDtypeStruct((2, TOKENS, GROUP), BF16),
            jax.ShapeDtypeStruct((TOKENS, WIDTH), BF16),
        ],
        compiler_params=params(),
    )(*pieces, weight, gain, cosine, sine)


def query_kernel(gathered, weight, gain, cosine, sine, out):
    mixed = jnp.dot(gathered[...], weight[0], preferred_element_type=F32)
    out[...] = headed(mixed, gain[...], cosine[...], sine[...])


def project_query(gathered, weight, gain, cosine, sine):
    return pl.pallas_call(
        query_kernel,
        out_shape=jax.ShapeDtypeStruct((TOKENS, GROUP), BF16),
        compiler_params=params(),
    )(gathered, weight, gain, cosine, sine)


def attend_head(query, blocks, head, old):
    lanes = slice(head * HD, (head + 1) * HD)
    scores = [
        lax.dot_general(
            ref[0, :, lanes], query, (((1,), (1,)), ((), ())), preferred_element_type=F32
        )
        for ref in blocks
    ]
    top = functools.reduce(
        jnp.maximum, [jnp.max(score, axis=0, keepdims=True) for score in scores]
    )
    if old is not None:
        top = jnp.maximum(top, old[1])
    shift = top * SCALE2
    numerator = denominator = None
    if old is not None:
        fade = jnp.exp2((old[1] - top) * SCALE2)
        numerator, denominator = old[0] * fade, old[2] * fade
    for score, ref in zip(scores, blocks):
        raised = jnp.exp2(score * SCALE2 - shift)
        part = lax.dot_general(
            ref[1, :, lanes],
            raised.astype(BF16),
            (((0,), (0,)), ((), ())),
            preferred_element_type=F32,
        )
        weight = jnp.sum(raised, axis=0, keepdims=True)
        numerator = part if numerator is None else numerator + part
        denominator = weight if denominator is None else denominator + weight
    return numerator, top, denominator


def attend_kernel(count, fresh, tile, *refs):
    queries, blocks, refs = refs[0], refs[1 : 1 + count], refs[1 + count :]
    if not fresh:
        old_total, old_stat, refs = refs[0], refs[1], refs[2:]
    total, stat = refs

    def step(index, _):
        at = pl.ds(pl.multiple_of(index * tile, tile), tile)
        for head in range(HEADS):
            lanes = slice(head * HD, (head + 1) * HD)
            old = None
            if not fresh:
                old = (
                    old_total[lanes, at],
                    old_stat[head : head + 1, at],
                    old_stat[HEADS + head : HEADS + head + 1, at],
                )
            numerator, top, denominator = attend_head(queries[at, lanes], blocks, head, old)
            total[lanes, at] = numerator
            stat[head : head + 1, at] = top
            stat[HEADS + head : HEADS + head + 1, at] = denominator
        return 0

    lax.fori_loop(0, queries.shape[0] // tile, step, 0)


def attend(queries, blocks, state):
    count = queries.shape[0]
    return pl.pallas_call(
        functools.partial(attend_kernel, len(blocks), state is None, 512),
        out_shape=[
            jax.ShapeDtypeStruct((GROUP, count), F32),
            jax.ShapeDtypeStruct((8, count), F32),
        ],
        compiler_params=params(),
    )(queries, *blocks, *(() if state is None else state))


def pack_levels(levels):
    rows = []
    for level in levels:
        for _ in range(3):
            coarse = level.astype(BF16).astype(F32)
            rows.append(coarse)
            level = level - coarse
    rows.append(jnp.zeros((STATS - len(rows),) + levels[0].shape[1:], F32))
    return jnp.concatenate(rows, axis=0).astype(BF16)


def finish_kernel(slots, count, *refs):
    queries, blocks, refs = refs[0], refs[1 : 1 + count], refs[1 + count :]
    old_total, old_stat, refs = refs[0], refs[1], refs[2:]
    for slot, out in zip(slots, refs):
        at = slice(slot * TOKENS, (slot + 1) * TOKENS)
        levels = []
        for head in range(HEADS):
            lanes = slice(head * HD, (head + 1) * HD)
            old = (
                old_total[lanes, at],
                old_stat[head : head + 1, at],
                old_stat[HEADS + head : HEADS + head + 1, at],
            )
            numerator, top, denominator = attend_head(queries[at, lanes], blocks, head, old)
            out[lanes, :] = (numerator / denominator).astype(BF16)
            levels.append(top * SCALE2 + jnp.log2(denominator))
        out[GROUP:, :] = pack_levels(levels)


def finish(queries, blocks, state, slots):
    return pl.pallas_call(
        functools.partial(finish_kernel, slots, len(blocks)),
        out_shape=[jax.ShapeDtypeStruct((GROUP + STATS, TOKENS), BF16)] * len(slots),
        compiler_params=params(),
    )(queries, *blocks, *state)


def merged(parts):
    tails = [part[GROUP:].astype(F32) for part in parts]
    outs, levels = [], []
    for head in range(HEADS):
        lanes = slice(head * HD, (head + 1) * HD)
        first = 3 * head
        level = [
            tail[first : first + 1] + tail[first + 1 : first + 2] + tail[first + 2 : first + 3]
            for tail in tails
        ]
        top = functools.reduce(jnp.maximum, level)
        shares = [jnp.exp2(one - top) for one in level]
        whole_share = functools.reduce(jnp.add, shares)
        mixed = functools.reduce(
            jnp.add, [part[lanes].astype(F32) * share for part, share in zip(parts, shares)]
        )
        outs.append((mixed / whole_share).astype(BF16))
        levels.append(top + jnp.log2(whole_share))
    return outs, levels


def merge_kernel(mine, theirs, out):
    outs, levels = merged([mine[...], theirs[...]])
    for head in range(HEADS):
        out[head * HD : (head + 1) * HD, :] = outs[head]
    out[GROUP:, :] = pack_levels(levels)


def merge(mine, theirs):
    return pl.pallas_call(
        merge_kernel,
        out_shape=jax.ShapeDtypeStruct((GROUP + STATS, TOKENS), BF16),
        compiler_params=params(),
    )(mine, theirs)


def out_kernel(mine, theirs, across, weight, a0, a1, a2, a3, b0, b1):
    heads, _ = merged([mine[...], theirs[...], across[...]])
    attended = jnp.concatenate(heads, axis=0)
    over = (((0,), (0,)), ((), ()))
    left = lax.dot_general(attended, weight[:, :HALF], over, preferred_element_type=F32)
    for step, out in enumerate((a0, a1, a2, a3)):
        out[...] = left[step * PAIR : (step + 1) * PAIR].astype(BF16)
    right = lax.dot_general(attended, weight[:, HALF:], over, preferred_element_type=F32)
    for step in range(X):
        for side, out in enumerate((b0, b1)):
            start = step * PAIR + side * LOCAL
            out[step * LOCAL : (step + 1) * LOCAL, :] = right[start : start + LOCAL].astype(BF16)


def out_project(mine, theirs, across, weight):
    return pl.pallas_call(
        out_kernel,
        out_shape=[jax.ShapeDtypeStruct((PAIR, HALF), BF16)] * X
        + [jax.ShapeDtypeStruct((X * LOCAL, HALF), BF16)] * 2,
        compiler_params=params(),
    )(mine, theirs, across, weight)


def half_sum_kernel(a0, a1, a2, a3, b0, b1, keep_a, keep_b, send_a, send_1, send_2, send_3):
    wide = lambda ref: ref[...].astype(F32)
    total = (wide(a0) + wide(a1)) + (wide(a2) + wide(a3))
    keep_a[...] = total[:LOCAL]
    send_a[...] = total[LOCAL:].astype(BF16)
    both = wide(b0) + wide(b1)
    keep_b[...] = both[:LOCAL]
    for step, out in enumerate((send_1, send_2, send_3)):
        out[...] = both[(step + 1) * LOCAL : (step + 2) * LOCAL].astype(BF16)


def half_sum(parts):
    return pl.pallas_call(
        half_sum_kernel,
        out_shape=[jax.ShapeDtypeStruct((LOCAL, HALF), F32)] * 2
        + [jax.ShapeDtypeStruct((LOCAL, HALF), BF16)] * 4,
        compiler_params=params(),
    )(*parts)


def final_kernel(
    tokens, keep_a, keep_b, a, b1, b2, b3, gate, shift, scale, weight, bias, block_out, latent
):
    wide = lambda ref: ref[...].astype(F32)
    projected = jnp.concatenate(
        [keep_a[...] + wide(a), (keep_b[...] + wide(b1)) + (wide(b2) + wide(b3))], axis=1
    )
    result = (wide(tokens) + gate[...] * projected).astype(BF16)
    block_out[...] = result
    final_in = (normed(result.astype(F32)) * (1.0 + scale[...]) + shift[...]).astype(BF16)
    mixed = jnp.dot(final_in, weight[...], preferred_element_type=F32)
    latent[...] = (mixed + bias[...]).astype(BF16)


def final(tokens, parts, gate, shift, scale, weight, bias):
    return pl.pallas_call(
        final_kernel,
        out_shape=[
            jax.ShapeDtypeStruct((LOCAL, WIDTH), BF16),
            jax.ShapeDtypeStruct((LOCAL, bias.shape[1]), BF16),
        ],
        compiler_params=params(),
    )(tokens, *parts, gate, shift, scale, weight, bias)


def extended(block, sides, width):
    for axis, dim in sides:
        count = lax.axis_size(axis)
        place = lax.axis_index(axis)
        forward = [(i, i + 1) for i in range(count - 1)]
        backward = [(target, source) for source, target in forward]
        first = lax.slice_in_dim(block, 0, width, axis=dim)
        end = lax.slice_in_dim(block, block.shape[dim] - width, None, axis=dim)
        low, high = lax.optimization_barrier(
            (lax.ppermute(end, axis, forward), lax.ppermute(first, axis, backward))
        )
        low = jnp.where(place == 0, first, low)
        high = jnp.where(place == count - 1, end, high)
        block = jnp.concatenate([low, block, high], axis=dim)
    return block


def local(
    block_in,
    mod_shift,
    mod_scale,
    mod_gate,
    qkv_weight,
    q_gain,
    k_gain,
    out_weight,
    final_shift,
    final_scale,
    final_weight,
    final_bias,
    conv_weight,
    conv_bias,
):
    frames, rows, columns, width = block_in.shape
    tokens = block_in.reshape(LOCAL, WIDTH)
    row = lambda vector: vector.reshape(1, -1)
    left, right = modulate(tokens, row(mod_shift), row(mod_scale))
    across_left = send_uly(left, dy=1)
    rights = [right] + [send_uly(right, dx=step) for step in range(1, X)]
    pair = jnp.concatenate([left, across_left], axis=0)
    quad = jnp.concatenate(rights, axis=0)
    lefts = [pair] + [send_uly(pair, dx=step) for step in range(1, X)]
    weight = fetch(qkv_weight, across_left)
    pieces = lefts + [quad, send_uly(quad, dy=1)]
    cosine, sine = rope_tables()

    key_value, gathered = project_key_value(pieces, weight, row(k_gain), cosine, sine)
    low, high = send_blk(key_value, dz=1), send_blk(key_value, dz=-1)
    query = project_query(gathered, weight, row(q_gain), cosine, sine)
    near = jnp.concatenate([query, send_blk(query, dc=1)], axis=0)
    far = send_blk(near, dy=1)
    queries = jnp.concatenate([near[:TOKENS], far[:TOKENS], near[TOKENS:], far[TOKENS:]], axis=0)

    state = None
    waiting = [key_value]
    for _ in range(Z // 2 - 2):
        next_low, next_high = send_blk(low, dz=1), send_blk(high, dz=-1)
        state = attend(queries, waiting + [low, high], state)
        low, high, state = lax.optimization_barrier((next_low, next_high, state))
        waiting = []
    middle = TOKENS // 2
    ends = [send_blk(low[:, :middle], dz=1), send_blk(high[:, middle:], dz=-1)]
    state = attend(queries, [low, high], state)

    mine_far, theirs_far = finish(queries, ends, state, (1, 3))
    theirs_far = send_blk(theirs_far, dc=1)
    across = send_blk(merge(mine_far, theirs_far), dy=1)
    mine, theirs = finish(queries, ends, state, (0, 2))
    shares = out_project(mine, send_blk(theirs, dc=1), across, out_weight)
    sums = half_sum(
        [shares[0]]
        + [send_uly(shares[step], dx=-step) for step in range(1, X)]
        + [shares[X], send_uly(shares[X + 1], dy=1)]
    )
    parts = list(sums[:2]) + [send_uly(sums[2], dy=1)]
    parts += [send_uly(sums[2 + step], dx=-step) for step in range(1, X)]
    block_out, latent_tok = final(
        tokens,
        parts,
        row(mod_gate),
        row(final_shift),
        row(final_scale),
        final_weight,
        row(final_bias),
    )

    channels = final_bias.shape[0] // 4
    latent = (
        latent_tok.reshape(frames, rows, columns, channels, 2, 2)
        .transpose(0, 1, 4, 2, 5, 3)
        .reshape(frames, 2 * rows, 2 * columns, channels)
    )
    padded = extended(latent, (("blk", 1), ("uly", 2)), 1)
    padded = jnp.concatenate([padded[:1], padded[:1], padded], axis=0)
    windows = []
    for time_lag in range(3):
        for row_lag in range(3):
            for column_lag in range(3):
                windows.append(
                    padded[
                        time_lag : time_lag + frames,
                        row_lag : row_lag + 2 * rows,
                        column_lag : column_lag + 2 * columns,
                    ]
                )
    patches = jnp.concatenate(windows, axis=-1)
    kernel = conv_weight.reshape(27 * channels, conv_weight.shape[-1])
    conv_out = (jnp.dot(patches, kernel, preferred_element_type=F32) + conv_bias).astype(BF16)
    return (block_out.reshape(frames, rows, columns, width), conv_out)


def solution(mesh):
    in_specs = (
        P(None, "blk", "uly", None),
        P(),
        P(),
        P(),
        P(None, None, "uly"),
        P(),
        P(),
        P("uly", None),
        P(),
        P(),
        P(),
        P(),
        P(),
        P(),
    )
    out_specs = (P(None, "blk", "uly", None), P(None, "blk", "uly", None))
    return jax.shard_map(local, mesh=mesh, in_specs=in_specs, out_specs=out_specs, check_vma=False)
```

```python
import functools

import jax
import jax.numpy as jnp
import numpy as np
from jax import lax
from jax.experimental import pallas as pl
from jax.experimental.pallas import tpu as pltpu
from jax.sharding import PartitionSpec as P

HD = 128
RT = 16
RH = 56
Z = 8
X = 4
HEADS = 3
GROUP = HEADS * HD
WIDTH = 3072
LOCAL = 32
PAIR = 2 * LOCAL
TOKENS = X * PAIR
STATS = 16
HALF = WIDTH // 2
MINE = TOKENS // 2
ORDER = (0, 2, 1, 3)
SCALE2 = float(HD ** (-0.5) / np.log(2.0))
F32 = jnp.float32
BF16 = jnp.bfloat16


def params(mib=32):
    return pltpu.CompilerParams(vmem_limit_bytes=mib * 1024 * 1024)


def whole():
    return pl.BlockSpec(memory_space=pltpu.VMEM)


def full(shape):
    return pl.BlockSpec(shape, lambda *_: (0,) * len(shape))


def blk_pairs(dy, dz, dc):
    return [
        (y * 2 * Z + z * 2 + c, (y ^ dy) * 2 * Z + (z + dz) % Z * 2 + (c ^ dc))
        for y in range(2)
        for z in range(Z)
        for c in range(2)
    ]


def ring_pairs():
    return [
        (y * 2 * Z + z * 2 + c, y * 2 * Z + (z + 1 - 2 * c) % Z * 2 + c)
        for y in range(2)
        for z in range(Z)
        for c in range(2)
    ]


def uly_pairs(ex, ey):
    return [(x * 2 + y, (x ^ ex) * 2 + (y ^ ey)) for x in range(X) for y in range(2)]


def send_blk(value, dy=0, dz=0, dc=0):
    return lax.ppermute(value, "blk", blk_pairs(dy, dz, dc))


def send_ring(value):
    return lax.ppermute(value, "blk", ring_pairs())


def send_uly(value, ex=0, ey=0):
    return lax.ppermute(value, "uly", uly_pairs(ex, ey))


def send_both(value, dy, ex):
    count = X * 2
    pairs = [
        (b * count + u, to_b * count + to_u)
        for b, to_b in blk_pairs(dy, 0, 0)
        for u, to_u in uly_pairs(ex, 0)
    ]
    return lax.ppermute(value, ("blk", "uly"), pairs)


def normed(values):
    center = values - jnp.mean(values, axis=-1, keepdims=True)
    spread = jnp.mean(center * center, axis=-1, keepdims=True)
    return center * lax.rsqrt(spread + 1e-06)


def modulate_kernel(tokens, shift, scale, *halves):
    x_mod = (normed(tokens[...].astype(F32)) * (1.0 + scale[...]) + shift[...]).astype(BF16)
    halves[0][...] = x_mod[:, :HALF]
    halves[1][...] = x_mod[:, HALF:]


def modulate(tokens, shift, scale):
    return pl.pallas_call(
        modulate_kernel,
        grid=(1,),
        in_specs=[full((LOCAL, WIDTH)), full((1, WIDTH)), full((1, WIDTH))],
        out_specs=[full((LOCAL, HALF))] * 2,
        out_shape=[jax.ShapeDtypeStruct((LOCAL, HALF), BF16)] * 2,
        compiler_params=params(),
    )(tokens, shift, scale)


def fetch_kernel(weight, after, out, sem):
    copy = pltpu.make_async_copy(weight, out, sem)
    copy.start()
    copy.wait()


def fetch(weight, after):
    return pl.pallas_call(
        fetch_kernel,
        in_specs=[pl.BlockSpec(memory_space=pl.ANY)] * 2,
        out_specs=whole(),
        out_shape=jax.ShapeDtypeStruct(weight.shape, weight.dtype),
        scratch_shapes=[pltpu.SemaphoreType.DMA],
        compiler_params=params(),
    )(weight, after)


def rope_tables():
    uly = lax.axis_index("uly")
    lane = np.arange(HD)
    section = np.where(lane < RT, 0, np.where(lane < RT + RH, 1, 2))
    start = np.array([0, RT, RT + RH])[section]
    length = np.array([RT, RH, RH])[section]
    half = length // 2
    upper = (lane - start) >= half
    index = jnp.asarray((lane - start) % half, F32)
    rates = 256.0 ** (-2.0 * index / jnp.asarray(length, F32))
    place = jnp.arange(TOKENS, dtype=jnp.int32)
    slot, dy, within = place // PAIR, place // LOCAL % 2, place % LOCAL
    ex = slot % 2 * 2 + slot // 2
    member = ((uly // 2) ^ ex) * 2 + ((uly % 2) ^ dy)
    frames_at = within // 16
    rows_at = lax.axis_index("blk") * 2 + within // 8 % 2
    columns_at = member * 8 + within % 8
    where = jnp.where(
        section[None, :] == 0,
        frames_at[:, None],
        jnp.where(section[None, :] == 1, rows_at[:, None], columns_at[:, None]),
    ).astype(F32)
    angles = where * rates[None, :]
    sign = jnp.asarray(np.where(upper, 1.0, -1.0), F32)
    return jnp.cos(angles), jnp.sin(angles) * sign[None, :]


def rope_partner(values):
    lane = lax.broadcasted_iota(jnp.int32, values.shape, 1)
    time_half, space_half = RT // 2, RH // 2
    first = jnp.where(
        lane < time_half,
        pltpu.roll(values, HD - time_half, axis=1),
        pltpu.roll(values, time_half, axis=1),
    )
    low = (lane < RT + space_half) | ((lane >= RT + RH) & (lane < RT + RH + space_half))
    rest = jnp.where(
        low, pltpu.roll(values, HD - space_half, axis=1), pltpu.roll(values, space_half, axis=1)
    )
    return jnp.where(lane < RT, first, rest)


def headed(mixed, gain, cosine, sine):
    out = []
    for head in range(HEADS):
        one = mixed[:, head * HD : (head + 1) * HD]
        one = one * lax.rsqrt(jnp.mean(one * one, axis=-1, keepdims=True) + 1e-06) * gain
        out.append((one * cosine + rope_partner(one) * sine).astype(BF16))
    return jnp.concatenate(out, axis=1)


def key_value_kernel(a0, a1, a2, a3, b0, b1, weight, gain, cosine, sine, out, gathered):
    for step, ref in enumerate((a0, a1, a2, a3)):
        gathered[step * PAIR : (step + 1) * PAIR, :HALF] = ref[...]
        for side, other in enumerate((b0, b1)):
            start = step * PAIR + side * LOCAL
            gathered[start : start + LOCAL, HALF:] = other[step * LOCAL : (step + 1) * LOCAL, :]
    keys = jnp.dot(gathered[...], weight[1], preferred_element_type=F32)
    out[0] = headed(keys, gain[...], cosine[...], sine[...])
    out[1] = jnp.dot(gathered[...], weight[2], preferred_element_type=F32).astype(BF16)


def project_key_value(pieces, weight, gain, cosine, sine):
    return pl.pallas_call(
        key_value_kernel,
        out_shape=[
            jax.ShapeDtypeStruct((2, TOKENS, GROUP), BF16),
            jax.ShapeDtypeStruct((TOKENS, WIDTH), BF16),
        ],
        compiler_params=params(),
    )(*pieces, weight, gain, cosine, sine)


def query_kernel(gathered, weight, gain, cosine, sine, out):
    mixed = jnp.dot(gathered[...], weight[0], preferred_element_type=F32)
    out[...] = headed(mixed, gain[...], cosine[...], sine[...])


def project_query(gathered, weight, gain, cosine, sine):
    return pl.pallas_call(
        query_kernel,
        out_shape=jax.ShapeDtypeStruct((TOKENS, GROUP), BF16),
        compiler_params=params(),
    )(gathered, weight, gain, cosine, sine)


def attend_items(items, blocks):
    scores = [
        [
            lax.dot_general(
                ref[0, :, lanes], query, (((1,), (1,)), ((), ())), preferred_element_type=F32
            )
            for ref in blocks
        ]
        for query, lanes, _ in items
    ]
    tops = [
        functools.reduce(jnp.maximum, [jnp.max(part, axis=0, keepdims=True) for part in score])
        for score in scores
    ]
    tops = [
        top if old is None else jnp.maximum(top, old[1]) for top, (_, _, old) in zip(tops, items)
    ]
    raised = [
        [jnp.exp2(part * SCALE2 - top * SCALE2) for part in score]
        for score, top in zip(scores, tops)
    ]
    results = []
    for part, top, (_, lanes, old) in zip(raised, tops, items):
        denominator = functools.reduce(
            jnp.add, [jnp.sum(one, axis=0, keepdims=True) for one in part]
        )
        numerator = functools.reduce(
            jnp.add,
            [
                lax.dot_general(
                    ref[1, :, lanes],
                    one.astype(BF16),
                    (((0,), (0,)), ((), ())),
                    preferred_element_type=F32,
                )
                for one, ref in zip(part, blocks)
            ],
        )
        if old is not None:
            fade = jnp.exp2((old[1] - top) * SCALE2)
            numerator = numerator + old[0] * fade
            denominator = denominator + old[2] * fade
        results.append((numerator, top, denominator))
    return results


def head_lanes(head):
    return slice(head * HD, (head + 1) * HD)


def old_state(total, stat, head):
    return (
        total[head_lanes(head), :],
        stat[head : head + 1, :],
        stat[HEADS + head : HEADS + head + 1, :],
    )


def attend_kernel(count, fresh, *refs):
    queries, blocks, refs = refs[0], refs[1 : 1 + count], refs[1 + count :]
    if not fresh:
        old_total, old_stat, refs = refs[0], refs[1], refs[2:]
    total, stat = refs
    items = [
        (
            queries[:, head_lanes(head)],
            head_lanes(head),
            None if fresh else old_state(old_total, old_stat, head),
        )
        for head in range(HEADS)
    ]
    for head, (numerator, top, denominator) in enumerate(attend_items(items, blocks)):
        total[head_lanes(head), :] = numerator
        stat[head : head + 1, :] = top
        stat[HEADS + head : HEADS + head + 1, :] = denominator


def attend(queries, blocks, state):
    count = queries.shape[0]
    return pl.pallas_call(
        functools.partial(attend_kernel, len(blocks), state is None),
        out_shape=[
            jax.ShapeDtypeStruct((GROUP, count), F32),
            jax.ShapeDtypeStruct((8, count), F32),
        ],
        compiler_params=params(),
    )(queries, *blocks, *(() if state is None else state))


def pack_levels(levels):
    rows = []
    for level in levels:
        for _ in range(3):
            coarse = level.astype(BF16).astype(F32)
            rows.append(coarse)
            level = level - coarse
    rows.append(jnp.zeros((STATS - len(rows),) + levels[0].shape[1:], F32))
    return jnp.concatenate(rows, axis=0).astype(BF16)


def finish_kernel(count, *refs):
    queries, blocks, refs = refs[0], refs[1 : 1 + count], refs[1 + count :]
    old_total, old_stat, keep, send = refs
    items = [
        (queries[:, head_lanes(head)], head_lanes(head), old_state(old_total, old_stat, head))
        for head in range(HEADS)
    ]
    levels = []
    middle = 2 * TOKENS
    for head, (numerator, top, denominator) in enumerate(attend_items(items, blocks)):
        lanes = head_lanes(head)
        partial = (numerator / denominator).astype(BF16)
        keep[lanes, :] = partial[:, :middle]
        send[lanes, :] = partial[:, middle:]
        levels.append(top * SCALE2 + jnp.log2(denominator))
    packed = pack_levels(levels)
    keep[GROUP:, :] = packed[:, :middle]
    send[GROUP:, :] = packed[:, middle:]


def finish(queries, blocks, state):
    return pl.pallas_call(
        functools.partial(finish_kernel, len(blocks)),
        out_shape=[jax.ShapeDtypeStruct((GROUP + STATS, 2 * TOKENS), BF16)] * 2,
        compiler_params=params(),
    )(queries, *blocks, *state)


def merged(parts):
    tails = [part[GROUP:].astype(F32) for part in parts]
    outs, levels = [], []
    for head in range(HEADS):
        lanes = head_lanes(head)
        first = 3 * head
        level = [
            tail[first : first + 1] + tail[first + 1 : first + 2] + tail[first + 2 : first + 3]
            for tail in tails
        ]
        top = functools.reduce(jnp.maximum, level)
        shares = [jnp.exp2(one - top) for one in level]
        whole_share = functools.reduce(jnp.add, shares)
        mixed = functools.reduce(
            jnp.add, [part[lanes].astype(F32) * share for part, share in zip(parts, shares)]
        )
        outs.append((mixed / whole_share).astype(BF16))
        levels.append(top + jnp.log2(whole_share))
    return outs, levels


def merge_kernel(mine, theirs, *outs):
    heads, levels = merged([mine[...], theirs[...]])
    packed = pack_levels(levels)
    for index, out in enumerate(outs):
        lanes = slice(index * MINE, (index + 1) * MINE)
        for head in range(HEADS):
            out[head_lanes(head), :] = heads[head][:, lanes]
        out[GROUP:, :] = packed[:, lanes]


def merge(mine, theirs):
    return pl.pallas_call(
        merge_kernel,
        out_shape=[jax.ShapeDtypeStruct((GROUP + STATS, MINE), BF16)] * 4,
        compiler_params=params(),
    )(mine, theirs)


def out_kernel(mine, across, beside, beyond, weight, other_weight, keep, *sends):
    over = (((0,), (0,)), ((), ()))
    own = jnp.concatenate(merged([mine[...], across[...]])[0], axis=0)
    other = jnp.concatenate(merged([beside[...], beyond[...]])[0], axis=0)
    for start in range(0, WIDTH, HALF):
        lanes = slice(start, start + HALF)
        product = lax.dot_general(own, weight[:, lanes], over, preferred_element_type=F32)
        product += lax.dot_general(other, other_weight[:, lanes], over, preferred_element_type=F32)
        keep[:, lanes] = product[:LOCAL]
        for index, out in enumerate(sends):
            out[:, lanes] = product[(index + 1) * LOCAL : (index + 2) * LOCAL].astype(BF16)


def out_project(parts, weight, other_weight):
    return pl.pallas_call(
        out_kernel,
        out_shape=[jax.ShapeDtypeStruct((LOCAL, WIDTH), F32)]
        + [jax.ShapeDtypeStruct((LOCAL, WIDTH), BF16)] * 3,
        compiler_params=params(),
    )(*parts, weight, other_weight)


def final_kernel(
    tokens, keep, a, b, c, gate, shift, scale, weight, bias, block_out, latent
):
    wide = lambda ref: ref[...].astype(F32)
    projected = (keep[...] + wide(a)) + (wide(b) + wide(c))
    result = (wide(tokens) + gate[...] * projected).astype(BF16)
    block_out[...] = result
    final_in = (normed(result.astype(F32)) * (1.0 + scale[...]) + shift[...]).astype(BF16)
    mixed = jnp.dot(final_in, weight[...], preferred_element_type=F32)
    latent[...] = (mixed + bias[...]).astype(BF16)


def final(tokens, parts, gate, shift, scale, weight, bias):
    return pl.pallas_call(
        final_kernel,
        out_shape=[
            jax.ShapeDtypeStruct((LOCAL, WIDTH), BF16),
            jax.ShapeDtypeStruct((LOCAL, bias.shape[1]), BF16),
        ],
        compiler_params=params(),
    )(tokens, *parts, gate, shift, scale, weight, bias)


def row_halo(first, end):
    place = lax.axis_index("blk")
    count = lax.axis_size("blk")
    odd = place % 2 == 1
    inner = lax.ppermute(jnp.where(odd, first, end), "blk", [(i, i ^ 1) for i in range(count)])
    links = [(i, i + 1) for i in range(1, count - 1, 2)]
    outer = lax.ppermute(
        jnp.where(odd, end, first), "blk", links + [(target, source) for source, target in links]
    )
    inner, outer = lax.optimization_barrier((inner, outer))
    low = jnp.where(place == 0, first, jnp.where(odd, inner, outer))
    high = jnp.where(place == count - 1, end, jnp.where(odd, outer, inner))
    return low, high


def column_halo(first, end):
    place = lax.axis_index("uly")
    count = lax.axis_size("uly")
    forward = [(i, i + 1) for i in range(count - 1)]
    backward = [(target, source) for source, target in forward]
    low, high = lax.optimization_barrier(
        (lax.ppermute(end, "uly", forward), lax.ppermute(first, "uly", backward))
    )
    return jnp.where(place == 0, first, low), jnp.where(place == count - 1, end, high)


def local(
    block_in,
    mod_shift,
    mod_scale,
    mod_gate,
    qkv_weight,
    q_gain,
    k_gain,
    out_weight,
    final_shift,
    final_scale,
    final_weight,
    final_bias,
    conv_weight,
    conv_bias,
):
    frames, rows, columns, width = block_in.shape
    tokens = block_in.reshape(LOCAL, WIDTH)
    core = lax.axis_index("blk") % 2
    row = lambda vector: vector.reshape(1, -1)
    left, right = modulate(tokens, row(mod_shift), row(mod_scale))
    across_left = send_uly(left, ey=1)
    rights = [right] + [send_uly(right, ex=ex) for ex in ORDER[1:]]
    pair = jnp.concatenate([left, across_left], axis=0)
    quad = jnp.concatenate(rights, axis=0)
    lefts = [pair] + [send_uly(pair, ex=ex) for ex in ORDER[1:]]
    weight = fetch(qkv_weight, across_left)
    pieces = lefts + [quad, send_uly(quad, ey=1)]
    cosine, sine = rope_tables()

    key_value, gathered = project_key_value(pieces, weight, row(k_gain), cosine, sine)
    near_chain, far_chain = key_value, send_blk(key_value, dc=1)
    blocks = [send_ring(near_chain), send_ring(far_chain)]
    gathered, _ = lax.optimization_barrier((gathered, far_chain))
    query = project_query(gathered, weight, row(q_gain), cosine, sine)
    near = jnp.concatenate([query, send_blk(query, dc=1)], axis=0)
    half = lax.dynamic_slice_in_dim(out_weight, core * (GROUP // 2), GROUP // 2, 0)
    near, half = lax.optimization_barrier((near, half))
    far = send_blk(near, dy=1)
    half = send_uly(half, ex=1)
    queries = jnp.concatenate([near[:TOKENS], far[:TOKENS], near[TOKENS:], far[TOKENS:]], axis=0)

    state = attend(queries, [key_value] + blocks, None)
    blocks = [send_ring(block) for block in blocks]
    later, state = lax.optimization_barrier((blocks[1], state))
    state = attend(queries, [blocks[0], later], state)
    blocks = [send_ring(blocks[0]), send_ring(later)]
    last, state = lax.optimization_barrier((blocks[0], state))
    state = attend(queries, [last, blocks[1]], state)
    last = send_ring(last)

    mine, theirs = finish(queries, [last], state)
    mine, beside, across, beyond = merge(mine, send_blk(theirs, dc=1))
    half, beside = lax.optimization_barrier((half, beside))
    other_half = send_blk(half, dc=1)
    other_weight = jnp.where(
        core == 0,
        jnp.concatenate([half, other_half], axis=0),
        jnp.concatenate([other_half, half], axis=0),
    )
    parts = [mine, send_blk(across, dy=1), send_uly(beside, ex=1), send_both(beyond, 1, 1)]
    shares = out_project(parts, out_weight, other_weight)
    parts = [
        shares[0],
        send_uly(shares[1], ey=1),
        send_uly(shares[2], ex=2),
        send_uly(shares[3], ex=2, ey=1),
    ]
    block_out, latent_tok = final(
        tokens,
        parts,
        row(mod_gate),
        row(final_shift),
        row(final_scale),
        final_weight,
        row(final_bias),
    )

    channels = final_bias.shape[0] // 4
    latent = (
        latent_tok.reshape(frames, rows, columns, channels, 2, 2)
        .transpose(0, 1, 4, 2, 5, 3)
        .reshape(frames, 2 * rows, 2 * columns, channels)
    )
    low, high = row_halo(latent[:, :1], latent[:, -1:])
    padded = jnp.concatenate([low, latent, high], axis=1)
    low, high = column_halo(padded[:, :, :1], padded[:, :, -1:])
    padded = jnp.concatenate([low, padded, high], axis=2)
    padded = jnp.concatenate([padded[:1], padded[:1], padded], axis=0)
    windows = []
    for time_lag in range(3):
        for row_lag in range(3):
            for column_lag in range(3):
                windows.append(
                    padded[
                        time_lag : time_lag + frames,
                        row_lag : row_lag + 2 * rows,
                        column_lag : column_lag + 2 * columns,
                    ]
                )
    patches = jnp.concatenate(windows, axis=-1)
    kernel = conv_weight.reshape(27 * channels, conv_weight.shape[-1])
    conv_out = (jnp.dot(patches, kernel, preferred_element_type=F32) + conv_bias).astype(BF16)
    return (block_out.reshape(frames, rows, columns, width), conv_out)


def solution(mesh):
    in_specs = (
        P(None, "blk", "uly", None),
        P(),
        P(),
        P(),
        P(None, None, "uly"),
        P(),
        P(),
        P("uly", None),
        P(),
        P(),
        P(),
        P(),
        P(),
        P(),
    )
    out_specs = (P(None, "blk", "uly", None), P(None, "blk", "uly", None))
    return jax.shard_map(local, mesh=mesh, in_specs=in_specs, out_specs=out_specs, check_vma=False)
```

```python
import functools

import jax
import jax.numpy as jnp
import numpy as np
from jax import lax
from jax.experimental import pallas as pl
from jax.experimental.pallas import tpu as pltpu
from jax.sharding import PartitionSpec as P

HD = 128
RT = 16
RH = 56
Z = 8
X = 4
HEADS = 3
GROUP = HEADS * HD
WIDTH = 3072
LOCAL = 32
PAIR = 2 * LOCAL
TOKENS = X * PAIR
STATS = 16
HALF = WIDTH // 2
MINE = TOKENS // 2
ORDER = (0, 3, 1, 2)
SCALE2 = float(HD ** (-0.5) / np.log(2.0))
F32 = jnp.float32
BF16 = jnp.bfloat16


def params(mib):
    return pltpu.CompilerParams(vmem_limit_bytes=mib * 1024 * 1024)


def whole():
    return pl.BlockSpec(memory_space=pltpu.VMEM)


def full(shape):
    return pl.BlockSpec(shape, lambda *_: (0,) * len(shape))


def blk_pairs(dy, dz, dc):
    return [
        (y * 2 * Z + z * 2 + c, (y ^ dy) * 2 * Z + (z + dz) % Z * 2 + (c ^ dc))
        for y in range(2)
        for z in range(Z)
        for c in range(2)
    ]


def ring_pairs():
    return [
        (y * 2 * Z + z * 2 + c, y * 2 * Z + (z + 1 - 2 * c) % Z * 2 + c)
        for y in range(2)
        for z in range(Z)
        for c in range(2)
    ]


def uly_pairs(ex, ey):
    return [(x * 2 + y, (x ^ ex) * 2 + (y ^ ey)) for x in range(X) for y in range(2)]


def send_blk(value, dy=0, dz=0, dc=0):
    return lax.ppermute(value, "blk", blk_pairs(dy, dz, dc))


def send_ring(value):
    return lax.ppermute(value, "blk", ring_pairs())


def send_uly(value, ex=0, ey=0):
    return lax.ppermute(value, "uly", uly_pairs(ex, ey))


def send_both(value, dy, ex):
    count = X * 2
    pairs = [
        (b * count + u, to_b * count + to_u)
        for b, to_b in blk_pairs(dy, 0, 0)
        for u, to_u in uly_pairs(ex, 0)
    ]
    return lax.ppermute(value, ("blk", "uly"), pairs)


def normed(values):
    center = values - jnp.mean(values, axis=-1, keepdims=True)
    spread = jnp.mean(center * center, axis=-1, keepdims=True)
    return center * lax.rsqrt(spread + 1e-06)


def modulate_kernel(tokens, shift, scale, *halves):
    x_mod = (normed(tokens[...].astype(F32)) * (1.0 + scale[...]) + shift[...]).astype(BF16)
    halves[0][...] = x_mod[:, :HALF]
    halves[1][...] = x_mod[:, HALF:]


def modulate(tokens, shift, scale):
    return pl.pallas_call(
        modulate_kernel,
        grid=(1,),
        in_specs=[full((LOCAL, WIDTH)), full((1, WIDTH)), full((1, WIDTH))],
        out_specs=[full((LOCAL, HALF))] * 2,
        out_shape=[jax.ShapeDtypeStruct((LOCAL, HALF), BF16)] * 2,
        compiler_params=params(4),
    )(tokens, shift, scale)


def fetch_kernel(weight, after, query, key_value, sems):
    copies = [
        pltpu.make_async_copy(weight.at[0], query, sems.at[0]),
        pltpu.make_async_copy(weight.at[pl.ds(1, 2)], key_value, sems.at[1]),
    ]
    for copy in copies:
        copy.start()
    for copy in copies:
        copy.wait()


def fetch(weight, after):
    return pl.pallas_call(
        fetch_kernel,
        in_specs=[pl.BlockSpec(memory_space=pl.ANY)] * 2,
        out_specs=[whole(), whole()],
        out_shape=[
            jax.ShapeDtypeStruct((WIDTH, GROUP), BF16),
            jax.ShapeDtypeStruct((2, WIDTH, GROUP), BF16),
        ],
        scratch_shapes=[pltpu.SemaphoreType.DMA((2,))],
        compiler_params=params(2),
    )(weight, after)


def rope_tables():
    uly = lax.axis_index("uly")
    lane = np.arange(HD)
    section = np.where(lane < RT, 0, np.where(lane < RT + RH, 1, 2))
    start = np.array([0, RT, RT + RH])[section]
    length = np.array([RT, RH, RH])[section]
    half = length // 2
    upper = (lane - start) >= half
    index = jnp.asarray((lane - start) % half, F32)
    rates = 256.0 ** (-2.0 * index / jnp.asarray(length, F32))
    place = jnp.arange(TOKENS, dtype=jnp.int32)
    slot, dy, within = place // PAIR, place // LOCAL % 2, place % LOCAL
    ex = jnp.where(slot == 0, 0, (slot + 1) % 3 + 1)
    member = ((uly // 2) ^ ex) * 2 + ((uly % 2) ^ dy)
    frames_at = within // 16
    rows_at = lax.axis_index("blk") * 2 + within // 8 % 2
    columns_at = member * 8 + within % 8
    where = jnp.where(
        section[None, :] == 0,
        frames_at[:, None],
        jnp.where(section[None, :] == 1, rows_at[:, None], columns_at[:, None]),
    ).astype(F32)
    angles = where * rates[None, :]
    sign = jnp.asarray(np.where(upper, 1.0, -1.0), F32)
    return jnp.cos(angles), jnp.sin(angles) * sign[None, :]


def rope_partner(values):
    lane = lax.broadcasted_iota(jnp.int32, values.shape, 1)
    time_half, space_half = RT // 2, RH // 2
    first = jnp.where(
        lane < time_half,
        pltpu.roll(values, HD - time_half, axis=1),
        pltpu.roll(values, time_half, axis=1),
    )
    low = (lane < RT + space_half) | ((lane >= RT + RH) & (lane < RT + RH + space_half))
    rest = jnp.where(
        low, pltpu.roll(values, HD - space_half, axis=1), pltpu.roll(values, space_half, axis=1)
    )
    return jnp.where(lane < RT, first, rest)


def headed(mixed, gain, cosine, sine):
    out = []
    for head in range(HEADS):
        one = mixed[:, head * HD : (head + 1) * HD]
        one = one * lax.rsqrt(jnp.mean(one * one, axis=-1, keepdims=True) + 1e-06) * gain
        out.append((one * cosine + rope_partner(one) * sine).astype(BF16))
    return jnp.concatenate(out, axis=1)


def key_value_kernel(a0, a1, a2, a3, b0, b1, weight, gain, cosine, sine, out, gathered):
    for step, ref in enumerate((a0, a1, a2, a3)):
        gathered[step * PAIR : (step + 1) * PAIR, :HALF] = ref[...]
        for side, other in enumerate((b0, b1)):
            start = step * PAIR + side * LOCAL
            gathered[start : start + LOCAL, HALF:] = other[step * LOCAL : (step + 1) * LOCAL, :]
    keys = jnp.dot(gathered[...], weight[0], preferred_element_type=F32)
    out[0] = headed(keys, gain[...], cosine[...], sine[...])
    out[1] = jnp.dot(gathered[...], weight[1], preferred_element_type=F32).astype(BF16)


def project_key_value(pieces, weight, gain, cosine, sine):
    return pl.pallas_call(
        key_value_kernel,
        out_shape=[
            jax.ShapeDtypeStruct((2, TOKENS, GROUP), BF16),
            jax.ShapeDtypeStruct((TOKENS, WIDTH), BF16),
        ],
        compiler_params=params(8),
    )(*pieces, weight, gain, cosine, sine)


def query_kernel(gathered, weight, gain, cosine, sine, out):
    mixed = jnp.dot(gathered[...], weight[...], preferred_element_type=F32)
    out[...] = headed(mixed, gain[...], cosine[...], sine[...])


def project_query(gathered, weight, gain, cosine, sine):
    return pl.pallas_call(
        query_kernel,
        out_shape=jax.ShapeDtypeStruct((TOKENS, GROUP), BF16),
        compiler_params=params(6),
    )(gathered, weight, gain, cosine, sine)


def attend_items(items, blocks):
    scores = [
        [
            lax.dot_general(
                ref[0, :, lanes], query, (((1,), (1,)), ((), ())), preferred_element_type=F32
            )
            for ref in blocks
        ]
        for query, lanes, _ in items
    ]
    tops = [
        functools.reduce(jnp.maximum, [jnp.max(part, axis=0, keepdims=True) for part in score])
        for score in scores
    ]
    tops = [
        top if old is None else jnp.maximum(top, old[1]) for top, (_, _, old) in zip(tops, items)
    ]
    raised = [
        [jnp.exp2(part * SCALE2 - top * SCALE2) for part in score]
        for score, top in zip(scores, tops)
    ]
    results = []
    for part, top, (_, lanes, old) in zip(raised, tops, items):
        denominator = functools.reduce(
            jnp.add, [jnp.sum(one, axis=0, keepdims=True) for one in part]
        )
        numerator = functools.reduce(
            jnp.add,
            [
                lax.dot_general(
                    ref[1, :, lanes],
                    one.astype(BF16),
                    (((0,), (0,)), ((), ())),
                    preferred_element_type=F32,
                )
                for one, ref in zip(part, blocks)
            ],
        )
        if old is not None:
            fade = jnp.exp2((old[1] - top) * SCALE2)
            numerator = numerator + old[0] * fade
            denominator = denominator + old[2] * fade
        results.append((numerator, top, denominator))
    return results


def head_lanes(head):
    return slice(head * HD, (head + 1) * HD)


def old_state(total, stat, head):
    return (
        total[head_lanes(head), :],
        stat[head : head + 1, :],
        stat[HEADS + head : HEADS + head + 1, :],
    )


def attend_kernel(count, fresh, *refs):
    queries, blocks, refs = refs[0], refs[1 : 1 + count], refs[1 + count :]
    if not fresh:
        old_total, old_stat, refs = refs[0], refs[1], refs[2:]
    total, stat = refs
    items = [
        (
            queries[:, head_lanes(head)],
            head_lanes(head),
            None if fresh else old_state(old_total, old_stat, head),
        )
        for head in range(HEADS)
    ]
    for head, (numerator, top, denominator) in enumerate(attend_items(items, blocks)):
        total[head_lanes(head), :] = numerator
        stat[head : head + 1, :] = top
        stat[HEADS + head : HEADS + head + 1, :] = denominator


def attend(queries, blocks, state):
    count = queries.shape[0]
    return pl.pallas_call(
        functools.partial(attend_kernel, len(blocks), state is None),
        out_shape=[
            jax.ShapeDtypeStruct((GROUP, count), F32),
            jax.ShapeDtypeStruct((8, count), F32),
        ],
        compiler_params=params(28),
    )(queries, *blocks, *(() if state is None else state))


def pack_levels(levels):
    rows = []
    for level in levels:
        for _ in range(3):
            coarse = level.astype(BF16).astype(F32)
            rows.append(coarse)
            level = level - coarse
    rows.append(jnp.zeros((STATS - len(rows),) + levels[0].shape[1:], F32))
    return jnp.concatenate(rows, axis=0).astype(BF16)


def finish_kernel(count, *refs):
    queries, blocks, refs = refs[0], refs[1 : 1 + count], refs[1 + count :]
    old_total, old_stat, keep, send = refs
    items = [
        (queries[:, head_lanes(head)], head_lanes(head), old_state(old_total, old_stat, head))
        for head in range(HEADS)
    ]
    levels = []
    middle = 2 * TOKENS
    for head, (numerator, top, denominator) in enumerate(attend_items(items, blocks)):
        lanes = head_lanes(head)
        partial = (numerator / denominator).astype(BF16)
        keep[lanes, :] = partial[:, :middle]
        send[lanes, :] = partial[:, middle:]
        levels.append(top * SCALE2 + jnp.log2(denominator))
    packed = pack_levels(levels)
    keep[GROUP:, :] = packed[:, :middle]
    send[GROUP:, :] = packed[:, middle:]


def finish(queries, blocks, state):
    return pl.pallas_call(
        functools.partial(finish_kernel, len(blocks)),
        out_shape=[jax.ShapeDtypeStruct((GROUP + STATS, 2 * TOKENS), BF16)] * 2,
        compiler_params=params(20),
    )(queries, *blocks, *state)


def merged(parts):
    tails = [part[GROUP:].astype(F32) for part in parts]
    outs, levels = [], []
    for head in range(HEADS):
        lanes = head_lanes(head)
        first = 3 * head
        level = [
            tail[first : first + 1] + tail[first + 1 : first + 2] + tail[first + 2 : first + 3]
            for tail in tails
        ]
        top = functools.reduce(jnp.maximum, level)
        shares = [jnp.exp2(one - top) for one in level]
        whole_share = functools.reduce(jnp.add, shares)
        mixed = functools.reduce(
            jnp.add, [part[lanes].astype(F32) * share for part, share in zip(parts, shares)]
        )
        outs.append((mixed / whole_share).astype(BF16))
        levels.append(top + jnp.log2(whole_share))
    return outs, levels


def merge_kernel(mine, theirs, *outs):
    heads, levels = merged([mine[...], theirs[...]])
    packed = pack_levels(levels)
    for index, out in enumerate(outs):
        lanes = slice(index * MINE, (index + 1) * MINE)
        for head in range(HEADS):
            out[head_lanes(head), :] = heads[head][:, lanes]
        out[GROUP:, :] = packed[:, lanes]


def merge(mine, theirs):
    return pl.pallas_call(
        merge_kernel,
        out_shape=[jax.ShapeDtypeStruct((GROUP + STATS, MINE), BF16)] * 4,
        compiler_params=params(6),
    )(mine, theirs)


def out_kernel(mine, across, beside, beyond, weight, half, other_half, core, keep, *sends):
    over = (((0,), (0,)), ((), ()))
    own = jnp.concatenate(merged([mine[...], across[...]])[0], axis=0)
    other = jnp.concatenate(merged([beside[...], beyond[...]])[0], axis=0).astype(F32)
    low, high = other[: GROUP // 2], other[GROUP // 2 :]
    first = core[...] < 0.5
    same = jnp.where(first, low, high).astype(BF16)
    swapped = jnp.where(first, high, low).astype(BF16)
    for start in range(0, WIDTH, HALF):
        lanes = slice(start, start + HALF)
        product = lax.dot_general(own, weight[:, lanes], over, preferred_element_type=F32)
        product += lax.dot_general(same, half[:, lanes], over, preferred_element_type=F32)
        product += lax.dot_general(swapped, other_half[:, lanes], over, preferred_element_type=F32)
        keep[:, lanes] = product[:LOCAL]
        for index, out in enumerate(sends):
            out[:, lanes] = product[(index + 1) * LOCAL : (index + 2) * LOCAL].astype(BF16)


def out_project(parts, weight, half, other_half, core):
    return pl.pallas_call(
        out_kernel,
        out_shape=[jax.ShapeDtypeStruct((LOCAL, WIDTH), F32)]
        + [jax.ShapeDtypeStruct((LOCAL, WIDTH), BF16)] * 3,
        compiler_params=params(10),
    )(*parts, weight, half, other_half, jnp.full((1, MINE), core, F32))


def final_kernel(
    tokens, keep, a, b, c, gate, shift, scale, weight, bias, block_out, latent
):
    wide = lambda ref: ref[...].astype(F32)
    projected = (keep[...] + wide(a)) + (wide(b) + wide(c))
    result = (wide(tokens) + gate[...] * projected).astype(BF16)
    block_out[...] = result
    final_in = (normed(result.astype(F32)) * (1.0 + scale[...]) + shift[...]).astype(BF16)
    mixed = jnp.dot(final_in, weight[...], preferred_element_type=F32)
    latent[...] = (mixed + bias[...]).astype(BF16)


def final(tokens, parts, gate, shift, scale, weight, bias):
    return pl.pallas_call(
        final_kernel,
        out_shape=[
            jax.ShapeDtypeStruct((LOCAL, WIDTH), BF16),
            jax.ShapeDtypeStruct((LOCAL, bias.shape[1]), BF16),
        ],
        compiler_params=params(6),
    )(tokens, *parts, gate, shift, scale, weight, bias)


def row_halo(first, end):
    place = lax.axis_index("blk")
    count = lax.axis_size("blk")
    odd = place % 2 == 1
    inner = lax.ppermute(jnp.where(odd, first, end), "blk", [(i, i ^ 1) for i in range(count)])
    links = [(i, i + 1) for i in range(1, count - 1, 2)]
    outer = lax.ppermute(
        jnp.where(odd, end, first), "blk", links + [(target, source) for source, target in links]
    )
    inner, outer = lax.optimization_barrier((inner, outer))
    low = jnp.where(place == 0, first, jnp.where(odd, inner, outer))
    high = jnp.where(place == count - 1, end, jnp.where(odd, outer, inner))
    return low, high


def column_halo(first, end):
    place = lax.axis_index("uly")
    count = lax.axis_size("uly")
    forward = [(i, i + 1) for i in range(count - 1)]
    backward = [(target, source) for source, target in forward]
    low, high = lax.optimization_barrier(
        (lax.ppermute(end, "uly", forward), lax.ppermute(first, "uly", backward))
    )
    return jnp.where(place == 0, first, low), jnp.where(place == count - 1, end, high)


def local(
    block_in,
    mod_shift,
    mod_scale,
    mod_gate,
    qkv_weight,
    q_gain,
    k_gain,
    out_weight,
    final_shift,
    final_scale,
    final_weight,
    final_bias,
    conv_weight,
    conv_bias,
):
    frames, rows, columns, width = block_in.shape
    tokens = block_in.reshape(LOCAL, WIDTH)
    core = lax.axis_index("blk") % 2
    row = lambda vector: vector.reshape(1, -1)
    left, right = modulate(tokens, row(mod_shift), row(mod_scale))
    across_left = send_uly(left, ey=1)
    rights = [right] + [send_uly(right, ex=ex) for ex in ORDER[1:]]
    pair = jnp.concatenate([left, across_left], axis=0)
    quad = jnp.concatenate(rights, axis=0)
    lefts = [pair] + [send_uly(pair, ex=ex) for ex in ORDER[1:]]
    query_weight, key_value_weight = fetch(qkv_weight, across_left)
    pieces = lefts + [quad, send_uly(quad, ey=1)]
    cosine, sine = rope_tables()

    key_value, gathered = project_key_value(pieces, key_value_weight, row(k_gain), cosine, sine)
    half = lax.dynamic_slice_in_dim(out_weight, core * (GROUP // 2), GROUP // 2, 0)
    near_chain, half = lax.optimization_barrier((key_value, half))
    far_chain = send_blk(near_chain, dc=1)
    half = send_uly(half, ex=1)
    blocks = [send_ring(near_chain), send_ring(far_chain)]
    gathered, _ = lax.optimization_barrier((gathered, far_chain))
    query = project_query(gathered, query_weight, row(q_gain), cosine, sine)
    near = jnp.concatenate([query, send_blk(query, dc=1)], axis=0)
    far = send_blk(near, dy=1)
    queries = jnp.concatenate([near[:TOKENS], far[:TOKENS], near[TOKENS:], far[TOKENS:]], axis=0)

    state = attend(queries, [key_value] + blocks, None)
    blocks = [send_ring(block) for block in blocks]
    later, state = lax.optimization_barrier((blocks[1], state))
    state = attend(queries, [blocks[0], later], state)
    blocks = [send_ring(blocks[0]), send_ring(later)]
    last, state = lax.optimization_barrier((blocks[0], state))
    state = attend(queries, [last, blocks[1]], state)
    last = send_ring(last)

    mine, theirs = finish(queries, [last], state)
    mine, beside, across, beyond = merge(mine, send_blk(theirs, dc=1))
    half, beside = lax.optimization_barrier((half, beside))
    other_half = send_blk(half, dc=1)
    parts = [mine, send_blk(across, dy=1), send_uly(beside, ex=1), send_both(beyond, 1, 1)]
    shares = out_project(parts, out_weight, half, other_half, core)
    parts = [
        shares[0],
        send_uly(shares[1], ey=1),
        send_uly(shares[2], ex=3),
        send_uly(shares[3], ex=3, ey=1),
    ]
    block_out, latent_tok = final(
        tokens,
        parts,
        row(mod_gate),
        row(final_shift),
        row(final_scale),
        final_weight,
        row(final_bias),
    )

    channels = final_bias.shape[0] // 4
    latent = (
        latent_tok.reshape(frames, rows, columns, channels, 2, 2)
        .transpose(0, 1, 4, 2, 5, 3)
        .reshape(frames, 2 * rows, 2 * columns, channels)
    )
    low, high = row_halo(latent[:, :1], latent[:, -1:])
    padded = jnp.concatenate([low, latent, high], axis=1)
    low, high = column_halo(padded[:, :, :1], padded[:, :, -1:])
    padded = jnp.concatenate([low, padded, high], axis=2)
    padded = jnp.concatenate([padded[:1], padded[:1], padded], axis=0)
    windows = []
    for time_lag in range(3):
        for row_lag in range(3):
            for column_lag in range(3):
                windows.append(
                    padded[
                        time_lag : time_lag + frames,
                        row_lag : row_lag + 2 * rows,
                        column_lag : column_lag + 2 * columns,
                    ]
                )
    patches = jnp.concatenate(windows, axis=-1)
    kernel = conv_weight.reshape(27 * channels, conv_weight.shape[-1])
    conv_out = (jnp.dot(patches, kernel, preferred_element_type=F32) + conv_bias).astype(BF16)
    return (block_out.reshape(frames, rows, columns, width), conv_out)


def solution(mesh):
    in_specs = (
        P(None, "blk", "uly", None),
        P(),
        P(),
        P(),
        P(None, None, "uly"),
        P(),
        P(),
        P("uly", None),
        P(),
        P(),
        P(),
        P(),
        P(),
        P(),
    )
    out_specs = (P(None, "blk", "uly", None), P(None, "blk", "uly", None))
    return jax.shard_map(local, mesh=mesh, in_specs=in_specs, out_specs=out_specs, check_vma=False)
```

```python
import functools

import jax
import jax.numpy as jnp
import numpy as np
from jax import lax
from jax.experimental import pallas as pl
from jax.experimental.pallas import tpu as pltpu
from jax.sharding import PartitionSpec as P

HD = 128
RT = 16
RH = 56
Z = 8
X = 4
HEADS = 3
GROUP = HEADS * HD
WIDTH = 3072
LOCAL = 32
PAIR = 2 * LOCAL
TOKENS = X * PAIR
STATS = 16
HALF = WIDTH // 2
MINE = TOKENS // 2
ORDER = (0, 3, 1, 2)
SCALE2 = float(HD ** (-0.5) / np.log(2.0))
F32 = jnp.float32
BF16 = jnp.bfloat16


def params(mib=12):
    return pltpu.CompilerParams(vmem_limit_bytes=mib * 1024 * 1024)


def whole():
    return pl.BlockSpec(memory_space=pltpu.VMEM)


def full(shape):
    return pl.BlockSpec(shape, lambda *_: (0,) * len(shape))


def blk_pairs(dy, dz, dc):
    return [
        (y * 2 * Z + z * 2 + c, (y ^ dy) * 2 * Z + (z + dz) % Z * 2 + (c ^ dc))
        for y in range(2)
        for z in range(Z)
        for c in range(2)
    ]


def ring_pairs():
    return [
        (y * 2 * Z + z * 2 + c, y * 2 * Z + (z + 1 - 2 * c) % Z * 2 + c)
        for y in range(2)
        for z in range(Z)
        for c in range(2)
    ]


def uly_pairs(ex, ey):
    return [(x * 2 + y, (x ^ ex) * 2 + (y ^ ey)) for x in range(X) for y in range(2)]


def send_blk(value, dy=0, dz=0, dc=0):
    return lax.ppermute(value, "blk", blk_pairs(dy, dz, dc))


def send_ring(value):
    return lax.ppermute(value, "blk", ring_pairs())


def send_uly(value, ex=0, ey=0):
    return lax.ppermute(value, "uly", uly_pairs(ex, ey))


def send_both(value, dy, ex):
    count = X * 2
    pairs = [
        (b * count + u, to_b * count + to_u)
        for b, to_b in blk_pairs(dy, 0, 0)
        for u, to_u in uly_pairs(ex, 0)
    ]
    return lax.ppermute(value, ("blk", "uly"), pairs)


def normed(values):
    center = values - jnp.mean(values, axis=-1, keepdims=True)
    spread = jnp.mean(center * center, axis=-1, keepdims=True)
    return center * lax.rsqrt(spread + 1e-06)


def modulate_kernel(tokens, scale_shift, left, right):
    scale, shift = scale_shift[0:1, :], scale_shift[1:2, :]
    x_mod = (normed(tokens[...].astype(F32)) * (1.0 + scale) + shift).astype(BF16)
    left[...] = x_mod[:, :HALF]
    right[...] = x_mod[:, HALF:]


def modulate(tokens, scale, shift):
    return pl.pallas_call(
        modulate_kernel,
        out_shape=[jax.ShapeDtypeStruct((LOCAL, HALF), BF16)] * 2,
        compiler_params=params(),
    )(tokens, jnp.stack([scale, shift]))


def fetch_kernel(weight, after, query, key_value, sems):
    copies = [
        pltpu.make_async_copy(weight.at[0], query, sems.at[0]),
        pltpu.make_async_copy(weight.at[pl.ds(1, 2)], key_value, sems.at[1]),
    ]
    for copy in copies:
        copy.start()
    for copy in copies:
        copy.wait()


def fetch(weight, after):
    return pl.pallas_call(
        fetch_kernel,
        in_specs=[pl.BlockSpec(memory_space=pl.ANY)] * 2,
        out_specs=[whole(), whole()],
        out_shape=[
            jax.ShapeDtypeStruct((WIDTH, GROUP), BF16),
            jax.ShapeDtypeStruct((2, WIDTH, GROUP), BF16),
        ],
        scratch_shapes=[pltpu.SemaphoreType.DMA((2,))],
        compiler_params=params(),
    )(weight, after)


def rope_tables():
    uly = lax.axis_index("uly")
    lane = np.arange(HD)
    section = np.where(lane < RT, 0, np.where(lane < RT + RH, 1, 2))
    start = np.array([0, RT, RT + RH])[section]
    length = np.array([RT, RH, RH])[section]
    half = length // 2
    upper = (lane - start) >= half
    index = jnp.asarray((lane - start) % half, F32)
    rates = 256.0 ** (-2.0 * index / jnp.asarray(length, F32))
    place = jnp.arange(TOKENS, dtype=jnp.int32)
    slot, dy, within = place // PAIR, place // LOCAL % 2, place % LOCAL
    ex = jnp.where(slot == 0, 0, (slot + 1) % 3 + 1)
    member = ((uly // 2) ^ ex) * 2 + ((uly % 2) ^ dy)
    frames_at = within // 16
    rows_at = lax.axis_index("blk") * 2 + within // 8 % 2
    columns_at = member * 8 + within % 8
    where = jnp.where(
        section[None, :] == 0,
        frames_at[:, None],
        jnp.where(section[None, :] == 1, rows_at[:, None], columns_at[:, None]),
    ).astype(F32)
    angles = where * rates[None, :]
    sign = jnp.asarray(np.where(upper, 1.0, -1.0), F32)
    return jnp.cos(angles), jnp.sin(angles) * sign[None, :]


def rope_partner(values):
    lane = lax.broadcasted_iota(jnp.int32, values.shape, 1)
    time_half, space_half = RT // 2, RH // 2
    first = jnp.where(
        lane < time_half,
        pltpu.roll(values, HD - time_half, axis=1),
        pltpu.roll(values, time_half, axis=1),
    )
    low = (lane < RT + space_half) | ((lane >= RT + RH) & (lane < RT + RH + space_half))
    rest = jnp.where(
        low, pltpu.roll(values, HD - space_half, axis=1), pltpu.roll(values, space_half, axis=1)
    )
    return jnp.where(lane < RT, first, rest)


def headed(mixed, gain, cosine, sine):
    out = []
    for head in range(HEADS):
        one = mixed[:, head * HD : (head + 1) * HD]
        one = one * lax.rsqrt(jnp.mean(one * one, axis=-1, keepdims=True) + 1e-06) * gain
        out.append((one * cosine + rope_partner(one) * sine).astype(BF16))
    return jnp.concatenate(out, axis=1)


def key_value_kernel(a0, a1, a2, a3, b0, b1, weight, gain, cosine, sine, out, gathered):
    for step, ref in enumerate((a0, a1, a2, a3)):
        gathered[step * PAIR : (step + 1) * PAIR, :HALF] = ref[...]
        for side, other in enumerate((b0, b1)):
            start = step * PAIR + side * LOCAL
            gathered[start : start + LOCAL, HALF:] = other[step * LOCAL : (step + 1) * LOCAL, :]
    keys = jnp.dot(gathered[...], weight[0], preferred_element_type=F32)
    out[0] = headed(keys, gain[...], cosine[...], sine[...])
    out[1] = jnp.dot(gathered[...], weight[1], preferred_element_type=F32).astype(BF16)


def project_key_value(pieces, weight, gain, cosine, sine):
    return pl.pallas_call(
        key_value_kernel,
        out_shape=[
            jax.ShapeDtypeStruct((2, TOKENS, GROUP), BF16),
            jax.ShapeDtypeStruct((TOKENS, WIDTH), BF16),
        ],
        compiler_params=params(),
    )(*pieces, weight, gain, cosine, sine)


def query_kernel(gathered, weight, gain, cosine, sine, out):
    mixed = jnp.dot(gathered[...], weight[...], preferred_element_type=F32)
    out[...] = headed(mixed, gain[...], cosine[...], sine[...])


def project_query(gathered, weight, gain, cosine, sine):
    return pl.pallas_call(
        query_kernel,
        out_shape=jax.ShapeDtypeStruct((TOKENS, GROUP), BF16),
        compiler_params=params(),
    )(gathered, weight, gain, cosine, sine)


def attend_items(items, blocks):
    scores = [
        [
            lax.dot_general(
                ref[0, :, lanes], query, (((1,), (1,)), ((), ())), preferred_element_type=F32
            )
            for ref in blocks
        ]
        for query, lanes, _ in items
    ]
    tops = [
        functools.reduce(jnp.maximum, [jnp.max(part, axis=0, keepdims=True) for part in score])
        for score in scores
    ]
    tops = [
        top if old is None else jnp.maximum(top, old[1]) for top, (_, _, old) in zip(tops, items)
    ]
    raised = [
        [jnp.exp2(part * SCALE2 - top * SCALE2) for part in score]
        for score, top in zip(scores, tops)
    ]
    results = []
    for part, top, (_, lanes, old) in zip(raised, tops, items):
        denominator = functools.reduce(
            jnp.add, [jnp.sum(one, axis=0, keepdims=True) for one in part]
        )
        numerator = functools.reduce(
            jnp.add,
            [
                lax.dot_general(
                    ref[1, :, lanes],
                    one.astype(BF16),
                    (((0,), (0,)), ((), ())),
                    preferred_element_type=F32,
                )
                for one, ref in zip(part, blocks)
            ],
        )
        if old is not None:
            fade = jnp.exp2((old[1] - top) * SCALE2)
            numerator = numerator + old[0] * fade
            denominator = denominator + old[2] * fade
        results.append((numerator, top, denominator))
    return results


def head_lanes(head):
    return slice(head * HD, (head + 1) * HD)


def old_state(total, stat, head):
    return (
        total[head_lanes(head), :],
        stat[head : head + 1, :],
        stat[HEADS + head : HEADS + head + 1, :],
    )


def attend_kernel(count, fresh, *refs):
    queries, blocks, refs = refs[0], refs[1 : 1 + count], refs[1 + count :]
    if not fresh:
        old_total, old_stat, refs = refs[0], refs[1], refs[2:]
    total, stat = refs
    items = [
        (
            queries[:, head_lanes(head)],
            head_lanes(head),
            None if fresh else old_state(old_total, old_stat, head),
        )
        for head in range(HEADS)
    ]
    for head, (numerator, top, denominator) in enumerate(attend_items(items, blocks)):
        total[head_lanes(head), :] = numerator
        stat[head : head + 1, :] = top
        stat[HEADS + head : HEADS + head + 1, :] = denominator


def attend(queries, blocks, state):
    count = queries.shape[0]
    return pl.pallas_call(
        functools.partial(attend_kernel, len(blocks), state is None),
        out_shape=[
            jax.ShapeDtypeStruct((GROUP, count), F32),
            jax.ShapeDtypeStruct((8, count), F32),
        ],
        compiler_params=params(),
    )(queries, *blocks, *(() if state is None else state))


def pack_levels(levels):
    rows = []
    for level in levels:
        for _ in range(3):
            coarse = level.astype(BF16).astype(F32)
            rows.append(coarse)
            level = level - coarse
    rows.append(jnp.zeros((STATS - len(rows),) + levels[0].shape[1:], F32))
    return jnp.concatenate(rows, axis=0).astype(BF16)


def finish_kernel(count, *refs):
    queries, blocks, refs = refs[0], refs[1 : 1 + count], refs[1 + count :]
    old_total, old_stat, keep, send = refs
    items = [
        (queries[:, head_lanes(head)], head_lanes(head), old_state(old_total, old_stat, head))
        for head in range(HEADS)
    ]
    levels = []
    middle = 2 * TOKENS
    for head, (numerator, top, denominator) in enumerate(attend_items(items, blocks)):
        lanes = head_lanes(head)
        partial = (numerator / denominator).astype(BF16)
        keep[lanes, :] = partial[:, :middle]
        send[lanes, :] = partial[:, middle:]
        levels.append(top * SCALE2 + jnp.log2(denominator))
    packed = pack_levels(levels)
    keep[GROUP:, :] = packed[:, :middle]
    send[GROUP:, :] = packed[:, middle:]


def finish(queries, blocks, state):
    return pl.pallas_call(
        functools.partial(finish_kernel, len(blocks)),
        out_shape=[jax.ShapeDtypeStruct((GROUP + STATS, 2 * TOKENS), BF16)] * 2,
        compiler_params=params(),
    )(queries, *blocks, *state)


def merged(parts):
    tails = [part[GROUP:].astype(F32) for part in parts]
    outs, levels = [], []
    for head in range(HEADS):
        lanes = head_lanes(head)
        first = 3 * head
        level = [
            tail[first : first + 1] + tail[first + 1 : first + 2] + tail[first + 2 : first + 3]
            for tail in tails
        ]
        top = functools.reduce(jnp.maximum, level)
        shares = [jnp.exp2(one - top) for one in level]
        whole_share = functools.reduce(jnp.add, shares)
        mixed = functools.reduce(
            jnp.add, [part[lanes].astype(F32) * share for part, share in zip(parts, shares)]
        )
        outs.append((mixed / whole_share).astype(BF16))
        levels.append(top + jnp.log2(whole_share))
    return outs, levels


def merge_kernel(mine, theirs, *outs):
    heads, levels = merged([mine[...], theirs[...]])
    packed = pack_levels(levels)
    for index, out in enumerate(outs):
        lanes = slice(index * MINE, (index + 1) * MINE)
        for head in range(HEADS):
            out[head_lanes(head), :] = heads[head][:, lanes]
        out[GROUP:, :] = packed[:, lanes]


def merge(mine, theirs):
    return pl.pallas_call(
        merge_kernel,
        out_shape=[jax.ShapeDtypeStruct((GROUP + STATS, MINE), BF16)] * 4,
        compiler_params=params(),
    )(mine, theirs)


def out_kernel(mine, across, beside, beyond, weight, other_weight, keep, *sends):
    over = (((0,), (0,)), ((), ()))
    own = jnp.concatenate(merged([mine[...], across[...]])[0], axis=0)
    other = jnp.concatenate(merged([beside[...], beyond[...]])[0], axis=0)
    for start in range(0, WIDTH, HALF):
        lanes = slice(start, start + HALF)
        product = lax.dot_general(own, weight[:, lanes], over, preferred_element_type=F32)
        product += lax.dot_general(other, other_weight[:, lanes], over, preferred_element_type=F32)
        keep[:, lanes] = product[:LOCAL]
        for index, out in enumerate(sends):
            out[:, lanes] = product[(index + 1) * LOCAL : (index + 2) * LOCAL].astype(BF16)


def out_project(parts, weight, other_weight):
    return pl.pallas_call(
        out_kernel,
        out_shape=[jax.ShapeDtypeStruct((LOCAL, WIDTH), F32)]
        + [jax.ShapeDtypeStruct((LOCAL, WIDTH), BF16)] * 3,
        compiler_params=params(),
    )(*parts, weight, other_weight)


def final_kernel(
    tokens, keep, a, b, c, gate, shift, scale, weight, bias, block_out, latent
):
    wide = lambda ref: ref[...].astype(F32)
    projected = (keep[...] + wide(a)) + (wide(b) + wide(c))
    result = (wide(tokens) + gate[...] * projected).astype(BF16)
    block_out[...] = result
    final_in = (normed(result.astype(F32)) * (1.0 + scale[...]) + shift[...]).astype(BF16)
    mixed = jnp.dot(final_in, weight[...], preferred_element_type=F32)
    latent[...] = (mixed + bias[...]).astype(BF16)


def final(tokens, parts, gate, shift, scale, weight, bias):
    return pl.pallas_call(
        final_kernel,
        out_shape=[
            jax.ShapeDtypeStruct((LOCAL, WIDTH), BF16),
            jax.ShapeDtypeStruct((LOCAL, bias.shape[1]), BF16),
        ],
        compiler_params=params(),
    )(tokens, *parts, gate, shift, scale, weight, bias)


def row_halo(first, end):
    place = lax.axis_index("blk")
    count = lax.axis_size("blk")
    odd = place % 2 == 1
    inner = lax.ppermute(jnp.where(odd, first, end), "blk", [(i, i ^ 1) for i in range(count)])
    links = [(i, i + 1) for i in range(1, count - 1, 2)]
    outer = lax.ppermute(
        jnp.where(odd, end, first), "blk", links + [(target, source) for source, target in links]
    )
    inner, outer = lax.optimization_barrier((inner, outer))
    low = jnp.where(place == 0, first, jnp.where(odd, inner, outer))
    high = jnp.where(place == count - 1, end, jnp.where(odd, outer, inner))
    return low, high


def column_halo(first, end):
    place = lax.axis_index("uly")
    count = lax.axis_size("uly")
    forward = [(i, i + 1) for i in range(count - 1)]
    backward = [(target, source) for source, target in forward]
    low, high = lax.optimization_barrier(
        (lax.ppermute(end, "uly", forward), lax.ppermute(first, "uly", backward))
    )
    return jnp.where(place == 0, first, low), jnp.where(place == count - 1, end, high)


def local(
    block_in,
    mod_shift,
    mod_scale,
    mod_gate,
    qkv_weight,
    q_gain,
    k_gain,
    out_weight,
    final_shift,
    final_scale,
    final_weight,
    final_bias,
    conv_weight,
    conv_bias,
):
    frames, rows, columns, width = block_in.shape
    tokens = block_in.reshape(LOCAL, WIDTH)
    core = lax.axis_index("blk") % 2
    row = lambda vector: vector.reshape(1, -1)
    left, right = modulate(tokens, mod_scale, mod_shift)
    across_left = send_uly(left, ey=1)
    rights = [right] + [send_uly(right, ex=ex) for ex in ORDER[1:]]
    pair = jnp.concatenate([left, across_left], axis=0)
    quad = jnp.concatenate(rights, axis=0)
    lefts = [pair] + [send_uly(pair, ex=ex) for ex in ORDER[1:]]
    query_weight, key_value_weight = fetch(qkv_weight, across_left)
    pieces = lefts + [quad, send_uly(quad, ey=1)]
    cosine, sine = rope_tables()

    key_value, gathered = project_key_value(pieces, key_value_weight, row(k_gain), cosine, sine)
    half = lax.dynamic_slice_in_dim(out_weight, core * (GROUP // 2), GROUP // 2, 0)
    near_chain, half = lax.optimization_barrier((key_value, half))
    far_chain = send_blk(near_chain, dc=1)
    half = send_uly(half, ex=1)
    blocks = [send_ring(near_chain), send_ring(far_chain)]
    gathered, _ = lax.optimization_barrier((gathered, far_chain))
    query = project_query(gathered, query_weight, row(q_gain), cosine, sine)
    near = jnp.concatenate([query, send_blk(query, dy=1)], axis=0)
    queries = jnp.concatenate([near, send_blk(near, dc=1)], axis=0)

    state = attend(queries, [key_value] + blocks, None)
    blocks = [send_ring(block) for block in blocks]
    later, state = lax.optimization_barrier((blocks[1], state))
    state = attend(queries, [blocks[0], later], state)
    blocks = [send_ring(blocks[0]), send_ring(later)]
    last, state = lax.optimization_barrier((blocks[0], state))
    state = attend(queries, [last, blocks[1]], state)
    last = send_ring(last)

    mine, theirs = finish(queries, [last], state)
    half, theirs = lax.optimization_barrier((half, theirs))
    mine, beside, across, beyond = merge(mine, send_blk(theirs, dc=1))
    half, beside = lax.optimization_barrier((half, beside))
    other_half = send_blk(half, dc=1)
    other_weight = jnp.where(
        core == 0,
        jnp.concatenate([half, other_half], axis=0),
        jnp.concatenate([other_half, half], axis=0),
    )
    parts = [mine, send_blk(across, dy=1), send_uly(beside, ex=1), send_both(beyond, 1, 1)]
    shares = out_project(parts, out_weight, other_weight)
    parts = [
        shares[0],
        send_uly(shares[1], ey=1),
        send_uly(shares[2], ex=3),
        send_uly(shares[3], ex=3, ey=1),
    ]
    block_out, latent_tok = final(
        tokens,
        parts,
        row(mod_gate),
        row(final_shift),
        row(final_scale),
        final_weight,
        row(final_bias),
    )

    channels = final_bias.shape[0] // 4
    latent = (
        latent_tok.reshape(frames, rows, columns, channels, 2, 2)
        .transpose(0, 1, 4, 2, 5, 3)
        .reshape(frames, 2 * rows, 2 * columns, channels)
    )
    low, high = row_halo(latent[:, :1], latent[:, -1:])
    padded = jnp.concatenate([low, latent, high], axis=1)
    low, high = column_halo(padded[:, :, :1], padded[:, :, -1:])
    padded = jnp.concatenate([low, padded, high], axis=2)
    padded = jnp.concatenate([padded[:1], padded[:1], padded], axis=0)
    windows = []
    for time_lag in range(3):
        for row_lag in range(3):
            for column_lag in range(3):
                windows.append(
                    padded[
                        time_lag : time_lag + frames,
                        row_lag : row_lag + 2 * rows,
                        column_lag : column_lag + 2 * columns,
                    ]
                )
    patches = jnp.concatenate(windows, axis=-1)
    kernel = conv_weight.reshape(27 * channels, conv_weight.shape[-1])
    conv_out = (jnp.dot(patches, kernel, preferred_element_type=F32) + conv_bias).astype(BF16)
    return (block_out.reshape(frames, rows, columns, width), conv_out)


def solution(mesh):
    in_specs = (
        P(None, "blk", "uly", None),
        P(),
        P(),
        P(),
        P(None, None, "uly"),
        P(),
        P(),
        P("uly", None),
        P(),
        P(),
        P(),
        P(),
        P(),
        P(),
    )
    out_specs = (P(None, "blk", "uly", None), P(None, "blk", "uly", None))
    return jax.shard_map(local, mesh=mesh, in_specs=in_specs, out_specs=out_specs, check_vma=False)
```

```python
import functools

import jax
import jax.numpy as jnp
import numpy as np
from jax import lax
from jax.experimental import pallas as pl
from jax.experimental.pallas import tpu as pltpu
from jax.sharding import PartitionSpec as P

HD = 128
RT = 16
RH = 56
Z = 8
X = 4
HEADS = 3
GROUP = HEADS * HD
WIDTH = 3072
LOCAL = 32
PAIR = 2 * LOCAL
TOKENS = X * PAIR
STATS = 16
HALF = WIDTH // 2
MINE = TOKENS // 2
ORDER = (0, 3, 1, 2)
SCALE2 = float(HD ** (-0.5) / np.log(2.0))
F32 = jnp.float32
BF16 = jnp.bfloat16


def params(mib=12):
    return pltpu.CompilerParams(vmem_limit_bytes=mib * 1024 * 1024)


def whole():
    return pl.BlockSpec(memory_space=pltpu.VMEM)


def full(shape):
    return pl.BlockSpec(shape, lambda *_: (0,) * len(shape))


def blk_pairs(dy, dz, dc):
    return [
        (y * 2 * Z + z * 2 + c, (y ^ dy) * 2 * Z + (z + dz) % Z * 2 + (c ^ dc))
        for y in range(2)
        for z in range(Z)
        for c in range(2)
    ]


def ring_pairs():
    return [
        (y * 2 * Z + z * 2 + c, y * 2 * Z + (z + 1 - 2 * c) % Z * 2 + c)
        for y in range(2)
        for z in range(Z)
        for c in range(2)
    ]


def uly_pairs(ex, ey):
    return [(x * 2 + y, (x ^ ex) * 2 + (y ^ ey)) for x in range(X) for y in range(2)]


def send_blk(value, dy=0, dz=0, dc=0):
    return lax.ppermute(value, "blk", blk_pairs(dy, dz, dc))


def send_ring(value):
    return lax.ppermute(value, "blk", ring_pairs())


def send_uly(value, ex=0, ey=0):
    return lax.ppermute(value, "uly", uly_pairs(ex, ey))


def spread_x(value):
    came = {ex: send_uly(value, ex=ex) for ex in (2, 3, 1)}
    return [came[ex] for ex in ORDER[1:]]


def send_both(value, dy, ex):
    count = X * 2
    pairs = [
        (b * count + u, to_b * count + to_u)
        for b, to_b in blk_pairs(dy, 0, 0)
        for u, to_u in uly_pairs(ex, 0)
    ]
    return lax.ppermute(value, ("blk", "uly"), pairs)


def normed(values):
    center = values - jnp.mean(values, axis=-1, keepdims=True)
    spread = jnp.mean(center * center, axis=-1, keepdims=True)
    return center * lax.rsqrt(spread + 1e-06)


def modulate_kernel(tokens, scale_shift, left, right):
    scale, shift = scale_shift[0:1, :], scale_shift[1:2, :]
    x_mod = (normed(tokens[...].astype(F32)) * (1.0 + scale) + shift).astype(BF16)
    left[...] = x_mod[:, :HALF]
    right[...] = x_mod[:, HALF:]


def modulate(tokens, scale, shift):
    return pl.pallas_call(
        modulate_kernel,
        out_shape=[jax.ShapeDtypeStruct((LOCAL, HALF), BF16)] * 2,
        compiler_params=params(),
    )(tokens, jnp.stack([scale, shift]))


def fetch_kernel(weight, after, query, key_value, sems):
    copies = [
        pltpu.make_async_copy(weight.at[0], query, sems.at[0]),
        pltpu.make_async_copy(weight.at[pl.ds(1, 2)], key_value, sems.at[1]),
    ]
    for copy in copies:
        copy.start()
    for copy in copies:
        copy.wait()


def fetch(weight, after):
    return pl.pallas_call(
        fetch_kernel,
        in_specs=[pl.BlockSpec(memory_space=pl.ANY)] * 2,
        out_specs=[whole(), whole()],
        out_shape=[
            jax.ShapeDtypeStruct((WIDTH, GROUP), BF16),
            jax.ShapeDtypeStruct((2, WIDTH, GROUP), BF16),
        ],
        scratch_shapes=[pltpu.SemaphoreType.DMA((2,))],
        compiler_params=params(),
    )(weight, after)


def rope_tables():
    uly = lax.axis_index("uly")
    lane = np.arange(HD)
    section = np.where(lane < RT, 0, np.where(lane < RT + RH, 1, 2))
    start = np.array([0, RT, RT + RH])[section]
    length = np.array([RT, RH, RH])[section]
    half = length // 2
    upper = (lane - start) >= half
    index = jnp.asarray((lane - start) % half, F32)
    rates = 256.0 ** (-2.0 * index / jnp.asarray(length, F32))
    place = jnp.arange(TOKENS, dtype=jnp.int32)
    slot, dy, within = place // PAIR, place // LOCAL % 2, place % LOCAL
    ex = jnp.where(slot == 0, 0, (slot + 1) % 3 + 1)
    member = ((uly // 2) ^ ex) * 2 + ((uly % 2) ^ dy)
    frames_at = within // 16
    rows_at = lax.axis_index("blk") * 2 + within // 8 % 2
    columns_at = member * 8 + within % 8
    where = jnp.where(
        section[None, :] == 0,
        frames_at[:, None],
        jnp.where(section[None, :] == 1, rows_at[:, None], columns_at[:, None]),
    ).astype(F32)
    angles = where * rates[None, :]
    sign = jnp.asarray(np.where(upper, 1.0, -1.0), F32)
    return jnp.cos(angles), jnp.sin(angles) * sign[None, :]


def rope_partner(values):
    lane = lax.broadcasted_iota(jnp.int32, values.shape, 1)
    time_half, space_half = RT // 2, RH // 2
    first = jnp.where(
        lane < time_half,
        pltpu.roll(values, HD - time_half, axis=1),
        pltpu.roll(values, time_half, axis=1),
    )
    low = (lane < RT + space_half) | ((lane >= RT + RH) & (lane < RT + RH + space_half))
    rest = jnp.where(
        low, pltpu.roll(values, HD - space_half, axis=1), pltpu.roll(values, space_half, axis=1)
    )
    return jnp.where(lane < RT, first, rest)


def headed(mixed, gain, cosine, sine):
    out = []
    for head in range(HEADS):
        one = mixed[:, head * HD : (head + 1) * HD]
        one = one * lax.rsqrt(jnp.mean(one * one, axis=-1, keepdims=True) + 1e-06) * gain
        out.append((one * cosine + rope_partner(one) * sine).astype(BF16))
    return jnp.concatenate(out, axis=1)


def key_value_kernel(a0, a1, a2, a3, b0, b1, weight, gain, cosine, sine, out, gathered):
    for step, ref in enumerate((a0, a1, a2, a3)):
        gathered[step * PAIR : (step + 1) * PAIR, :HALF] = ref[...]
        for side, other in enumerate((b0, b1)):
            start = step * PAIR + side * LOCAL
            gathered[start : start + LOCAL, HALF:] = other[step * LOCAL : (step + 1) * LOCAL, :]
    keys = jnp.dot(gathered[...], weight[0], preferred_element_type=F32)
    out[0] = headed(keys, gain[...], cosine[...], sine[...])
    out[1] = jnp.dot(gathered[...], weight[1], preferred_element_type=F32).astype(BF16)


def project_key_value(pieces, weight, gain, cosine, sine):
    return pl.pallas_call(
        key_value_kernel,
        out_shape=[
            jax.ShapeDtypeStruct((2, TOKENS, GROUP), BF16),
            jax.ShapeDtypeStruct((TOKENS, WIDTH), BF16),
        ],
        compiler_params=params(),
    )(*pieces, weight, gain, cosine, sine)


def query_kernel(gathered, weight, gain, cosine, sine, out):
    mixed = jnp.dot(gathered[...], weight[...], preferred_element_type=F32)
    out[...] = headed(mixed, gain[...], cosine[...], sine[...])


def project_query(gathered, weight, gain, cosine, sine):
    return pl.pallas_call(
        query_kernel,
        out_shape=jax.ShapeDtypeStruct((TOKENS, GROUP), BF16),
        compiler_params=params(),
    )(gathered, weight, gain, cosine, sine)


def attend_items(items, blocks):
    scores = [
        [
            lax.dot_general(
                ref[0, :, lanes], query, (((1,), (1,)), ((), ())), preferred_element_type=F32
            )
            for ref in blocks
        ]
        for query, lanes, _ in items
    ]
    tops = [
        functools.reduce(jnp.maximum, [jnp.max(part, axis=0, keepdims=True) for part in score])
        for score in scores
    ]
    tops = [
        top if old is None else jnp.maximum(top, old[1]) for top, (_, _, old) in zip(tops, items)
    ]
    raised = [
        [jnp.exp2(part * SCALE2 - top * SCALE2) for part in score]
        for score, top in zip(scores, tops)
    ]
    results = []
    for part, top, (_, lanes, old) in zip(raised, tops, items):
        denominator = functools.reduce(
            jnp.add, [jnp.sum(one, axis=0, keepdims=True) for one in part]
        )
        numerator = functools.reduce(
            jnp.add,
            [
                lax.dot_general(
                    ref[1, :, lanes],
                    one.astype(BF16),
                    (((0,), (0,)), ((), ())),
                    preferred_element_type=F32,
                )
                for one, ref in zip(part, blocks)
            ],
        )
        if old is not None:
            fade = jnp.exp2((old[1] - top) * SCALE2)
            numerator = numerator + old[0] * fade
            denominator = denominator + old[2] * fade
        results.append((numerator, top, denominator))
    return results


def head_lanes(head):
    return slice(head * HD, (head + 1) * HD)


def old_state(total, stat, head):
    return (
        total[head_lanes(head), :],
        stat[head : head + 1, :],
        stat[HEADS + head : HEADS + head + 1, :],
    )


def attend_kernel(count, fresh, *refs):
    queries, blocks, refs = refs[0], refs[1 : 1 + count], refs[1 + count :]
    if not fresh:
        old_total, old_stat, refs = refs[0], refs[1], refs[2:]
    total, stat = refs
    items = [
        (
            queries[:, head_lanes(head)],
            head_lanes(head),
            None if fresh else old_state(old_total, old_stat, head),
        )
        for head in range(HEADS)
    ]
    for head, (numerator, top, denominator) in enumerate(attend_items(items, blocks)):
        total[head_lanes(head), :] = numerator
        stat[head : head + 1, :] = top
        stat[HEADS + head : HEADS + head + 1, :] = denominator


def attend(queries, blocks, state):
    count = queries.shape[0]
    return pl.pallas_call(
        functools.partial(attend_kernel, len(blocks), state is None),
        out_shape=[
            jax.ShapeDtypeStruct((GROUP, count), F32),
            jax.ShapeDtypeStruct((8, count), F32),
        ],
        compiler_params=params(),
    )(queries, *blocks, *(() if state is None else state))


def pack_levels(levels):
    rows = []
    for level in levels:
        for _ in range(3):
            coarse = level.astype(BF16).astype(F32)
            rows.append(coarse)
            level = level - coarse
    rows.append(jnp.zeros((STATS - len(rows),) + levels[0].shape[1:], F32))
    return jnp.concatenate(rows, axis=0).astype(BF16)


def finish_kernel(count, *refs):
    queries, blocks, refs = refs[0], refs[1 : 1 + count], refs[1 + count :]
    old_total, old_stat, keep, send = refs
    items = [
        (queries[:, head_lanes(head)], head_lanes(head), old_state(old_total, old_stat, head))
        for head in range(HEADS)
    ]
    levels = []
    middle = 2 * TOKENS
    for head, (numerator, top, denominator) in enumerate(attend_items(items, blocks)):
        lanes = head_lanes(head)
        partial = (numerator / denominator).astype(BF16)
        keep[lanes, :] = partial[:, :middle]
        send[lanes, :] = partial[:, middle:]
        levels.append(top * SCALE2 + jnp.log2(denominator))
    packed = pack_levels(levels)
    keep[GROUP:, :] = packed[:, :middle]
    send[GROUP:, :] = packed[:, middle:]


def finish(queries, blocks, state):
    return pl.pallas_call(
        functools.partial(finish_kernel, len(blocks)),
        out_shape=[jax.ShapeDtypeStruct((GROUP + STATS, 2 * TOKENS), BF16)] * 2,
        compiler_params=params(),
    )(queries, *blocks, *state)


def merged(parts):
    tails = [part[GROUP:].astype(F32) for part in parts]
    outs, levels = [], []
    for head in range(HEADS):
        lanes = head_lanes(head)
        first = 3 * head
        level = [
            tail[first : first + 1] + tail[first + 1 : first + 2] + tail[first + 2 : first + 3]
            for tail in tails
        ]
        top = functools.reduce(jnp.maximum, level)
        shares = [jnp.exp2(one - top) for one in level]
        whole_share = functools.reduce(jnp.add, shares)
        mixed = functools.reduce(
            jnp.add, [part[lanes].astype(F32) * share for part, share in zip(parts, shares)]
        )
        outs.append((mixed / whole_share).astype(BF16))
        levels.append(top + jnp.log2(whole_share))
    return outs, levels


def merge_kernel(mine, theirs, *outs):
    heads, levels = merged([mine[...], theirs[...]])
    packed = pack_levels(levels)
    for index, out in enumerate(outs):
        lanes = slice(index * MINE, (index + 1) * MINE)
        for head in range(HEADS):
            out[head_lanes(head), :] = heads[head][:, lanes]
        out[GROUP:, :] = packed[:, lanes]


def merge(mine, theirs):
    return pl.pallas_call(
        merge_kernel,
        out_shape=[jax.ShapeDtypeStruct((GROUP + STATS, MINE), BF16)] * 4,
        compiler_params=params(),
    )(mine, theirs)


def out_kernel(mine, across, beside, beyond, weight, other_weight, keep, *sends):
    over = (((0,), (0,)), ((), ()))
    own = jnp.concatenate(merged([mine[...], across[...]])[0], axis=0)
    other = jnp.concatenate(merged([beside[...], beyond[...]])[0], axis=0)
    for start in range(0, WIDTH, HALF):
        lanes = slice(start, start + HALF)
        product = lax.dot_general(own, weight[:, lanes], over, preferred_element_type=F32)
        product += lax.dot_general(other, other_weight[:, lanes], over, preferred_element_type=F32)
        keep[:, lanes] = product[:LOCAL]
        for index, out in enumerate(sends):
            out[:, lanes] = product[(index + 1) * LOCAL : (index + 2) * LOCAL].astype(BF16)


def out_project(parts, weight, other_weight):
    return pl.pallas_call(
        out_kernel,
        out_shape=[jax.ShapeDtypeStruct((LOCAL, WIDTH), F32)]
        + [jax.ShapeDtypeStruct((LOCAL, WIDTH), BF16)] * 3,
        compiler_params=params(),
    )(*parts, weight, other_weight)


def final_kernel(
    tokens, keep, a, b, c, gate, shift, scale, weight, bias, block_out, latent
):
    wide = lambda ref: ref[...].astype(F32)
    projected = (keep[...] + wide(a)) + (wide(b) + wide(c))
    result = (wide(tokens) + gate[...] * projected).astype(BF16)
    block_out[...] = result
    final_in = (normed(result.astype(F32)) * (1.0 + scale[...]) + shift[...]).astype(BF16)
    mixed = jnp.dot(final_in, weight[...], preferred_element_type=F32)
    latent[...] = (mixed + bias[...]).astype(BF16)


def final(tokens, parts, gate, shift, scale, weight, bias):
    return pl.pallas_call(
        final_kernel,
        out_shape=[
            jax.ShapeDtypeStruct((LOCAL, WIDTH), BF16),
            jax.ShapeDtypeStruct((LOCAL, bias.shape[1]), BF16),
        ],
        compiler_params=params(),
    )(tokens, *parts, gate, shift, scale, weight, bias)


def halo(axis, first, end):
    place = lax.axis_index(axis)
    count = lax.axis_size(axis)
    odd = place % 2 == 1
    inner = lax.ppermute(jnp.where(odd, first, end), axis, [(i, i ^ 1) for i in range(count)])
    links = [(i, i + 1) for i in range(1, count - 1, 2)]
    outer = lax.ppermute(
        jnp.where(odd, end, first), axis, links + [(target, source) for source, target in links]
    )
    inner, outer = lax.optimization_barrier((inner, outer))
    low = jnp.where(place == 0, first, jnp.where(odd, inner, outer))
    high = jnp.where(place == count - 1, end, jnp.where(odd, outer, inner))
    return low, high


def local(
    block_in,
    mod_shift,
    mod_scale,
    mod_gate,
    qkv_weight,
    q_gain,
    k_gain,
    out_weight,
    final_shift,
    final_scale,
    final_weight,
    final_bias,
    conv_weight,
    conv_bias,
):
    frames, rows, columns, width = block_in.shape
    tokens = block_in.reshape(LOCAL, WIDTH)
    core = lax.axis_index("blk") % 2
    row = lambda vector: vector.reshape(1, -1)
    left, right = modulate(tokens, mod_scale, mod_shift)
    across_left = send_uly(left, ey=1)
    rights = [right] + spread_x(right)
    pair = jnp.concatenate([left, across_left], axis=0)
    quad = jnp.concatenate(rights, axis=0)
    lefts = [pair] + spread_x(pair)
    query_weight, key_value_weight = fetch(qkv_weight, across_left)
    pieces = lefts + [quad, send_uly(quad, ey=1)]
    cosine, sine = rope_tables()

    key_value, gathered = project_key_value(pieces, key_value_weight, row(k_gain), cosine, sine)
    half = lax.dynamic_slice_in_dim(out_weight, core * (GROUP // 2), GROUP // 2, 0)
    near_chain, half = lax.optimization_barrier((key_value, half))
    far_chain = send_blk(near_chain, dc=1)
    half = send_uly(half, ex=1)
    blocks = [send_ring(near_chain), send_ring(far_chain)]
    gathered, _ = lax.optimization_barrier((gathered, far_chain))
    query = project_query(gathered, query_weight, row(q_gain), cosine, sine)
    near = jnp.concatenate([query, send_blk(query, dy=1)], axis=0)
    queries = jnp.concatenate([near, send_blk(near, dc=1)], axis=0)

    state = attend(queries, [key_value] + blocks, None)
    blocks = [send_ring(block) for block in blocks]
    later, state = lax.optimization_barrier((blocks[1], state))
    state = attend(queries, [blocks[0], later], state)
    blocks = [send_ring(blocks[0]), send_ring(later)]
    last, state = lax.optimization_barrier((blocks[0], state))
    state = attend(queries, [last, blocks[1]], state)
    last = send_ring(last)

    mine, theirs = finish(queries, [last], state)
    half, theirs = lax.optimization_barrier((half, theirs))
    mine, beside, across, beyond = merge(mine, send_blk(theirs, dc=1))
    half, beside = lax.optimization_barrier((half, beside))
    other_half = send_blk(half, dc=1)
    other_weight = jnp.where(
        core == 0,
        jnp.concatenate([half, other_half], axis=0),
        jnp.concatenate([other_half, half], axis=0),
    )
    beyond = send_both(beyond, 1, 1)
    parts = [mine, send_blk(across, dy=1), send_uly(beside, ex=1), beyond]
    shares = out_project(parts, out_weight, other_weight)
    parts = [
        shares[0],
        send_uly(shares[3], ex=3, ey=1),
        send_uly(shares[2], ex=3),
        send_uly(shares[1], ey=1),
    ]
    block_out, latent_tok = final(
        tokens,
        parts,
        row(mod_gate),
        row(final_shift),
        row(final_scale),
        final_weight,
        row(final_bias),
    )

    channels = final_bias.shape[0] // 4
    latent = (
        latent_tok.reshape(frames, rows, columns, channels, 2, 2)
        .transpose(0, 1, 4, 2, 5, 3)
        .reshape(frames, 2 * rows, 2 * columns, channels)
    )
    low, high = halo("blk", latent[:, :1], latent[:, -1:])
    padded = jnp.concatenate([low, latent, high], axis=1)
    low, high = halo("uly", padded[:, :, :1], padded[:, :, -1:])
    padded = jnp.concatenate([low, padded, high], axis=2)
    padded = jnp.concatenate([padded[:1], padded[:1], padded], axis=0)
    windows = []
    for time_lag in range(3):
        for row_lag in range(3):
            for column_lag in range(3):
                windows.append(
                    padded[
                        time_lag : time_lag + frames,
                        row_lag : row_lag + 2 * rows,
                        column_lag : column_lag + 2 * columns,
                    ]
                )
    patches = jnp.concatenate(windows, axis=-1)
    kernel = conv_weight.reshape(27 * channels, conv_weight.shape[-1])
    conv_out = (jnp.dot(patches, kernel, preferred_element_type=F32) + conv_bias).astype(BF16)
    return (block_out.reshape(frames, rows, columns, width), conv_out)


def solution(mesh):
    in_specs = (
        P(None, "blk", "uly", None),
        P(),
        P(),
        P(),
        P(None, None, "uly"),
        P(),
        P(),
        P("uly", None),
        P(),
        P(),
        P(),
        P(),
        P(),
        P(),
    )
    out_specs = (P(None, "blk", "uly", None), P(None, "blk", "uly", None))
    return jax.shard_map(local, mesh=mesh, in_specs=in_specs, out_specs=out_specs, check_vma=False)
```

```python
import functools

import jax
import jax.numpy as jnp
import numpy as np
from jax import lax
from jax.experimental import pallas as pl
from jax.experimental.pallas import tpu as pltpu
from jax.sharding import PartitionSpec as P

HD = 128
RT = 16
RH = 56
Z = 8
X = 4
HEADS = 3
GROUP = HEADS * HD
WIDTH = 3072
LOCAL = 32
PAIR = 2 * LOCAL
TOKENS = X * PAIR
STATS = 16
HALF = WIDTH // 2
LEFT = 1280
RIGHT = WIDTH - LEFT
MINE = TOKENS // 2
ORDER = (0, 3, 1, 2)
SCALE2 = float(HD ** (-0.5) / np.log(2.0))
F32 = jnp.float32
BF16 = jnp.bfloat16


def params(mib=12):
    return pltpu.CompilerParams(vmem_limit_bytes=mib * 1024 * 1024)


def whole():
    return pl.BlockSpec(memory_space=pltpu.VMEM)


def full(shape):
    return pl.BlockSpec(shape, lambda *_: (0,) * len(shape))


def blk_pairs(dy, dz, dc):
    return [
        (y * 2 * Z + z * 2 + c, (y ^ dy) * 2 * Z + (z + dz) % Z * 2 + (c ^ dc))
        for y in range(2)
        for z in range(Z)
        for c in range(2)
    ]


def ring_pairs():
    return [
        (y * 2 * Z + z * 2 + c, y * 2 * Z + (z + 1 - 2 * c) % Z * 2 + c)
        for y in range(2)
        for z in range(Z)
        for c in range(2)
    ]


def uly_pairs(ex, ey):
    return [(x * 2 + y, (x ^ ex) * 2 + (y ^ ey)) for x in range(X) for y in range(2)]


def send_blk(value, dy=0, dz=0, dc=0):
    return lax.ppermute(value, "blk", blk_pairs(dy, dz, dc))


def send_ring(value):
    return lax.ppermute(value, "blk", ring_pairs())


def send_uly(value, ex=0, ey=0):
    return lax.ppermute(value, "uly", uly_pairs(ex, ey))


def spread_x(value):
    came = {ex: send_uly(value, ex=ex) for ex in (2, 3, 1)}
    return [came[ex] for ex in ORDER[1:]]


def send_both(value, dy, ex):
    count = X * 2
    pairs = [
        (b * count + u, to_b * count + to_u)
        for b, to_b in blk_pairs(dy, 0, 0)
        for u, to_u in uly_pairs(ex, 0)
    ]
    return lax.ppermute(value, ("blk", "uly"), pairs)


def normed(values):
    center = values - jnp.mean(values, axis=-1, keepdims=True)
    spread = jnp.mean(center * center, axis=-1, keepdims=True)
    return center * lax.rsqrt(spread + 1e-06)


def modulate_kernel(tokens, scale_shift, left, right):
    scale, shift = scale_shift[0:1, :], scale_shift[1:2, :]
    x_mod = (normed(tokens[...].astype(F32)) * (1.0 + scale) + shift).astype(BF16)
    left[...] = x_mod[:, :LEFT]
    right[...] = x_mod[:, LEFT:]


def modulate(tokens, scale, shift):
    return pl.pallas_call(
        modulate_kernel,
        out_shape=[
            jax.ShapeDtypeStruct((LOCAL, LEFT), BF16),
            jax.ShapeDtypeStruct((LOCAL, RIGHT), BF16),
        ],
        compiler_params=params(),
    )(tokens, jnp.stack([scale, shift]))


def fetch_kernel(weight, after, query, key_value, sems):
    copies = [
        pltpu.make_async_copy(weight.at[0], query, sems.at[0]),
        pltpu.make_async_copy(weight.at[pl.ds(1, 2)], key_value, sems.at[1]),
    ]
    for copy in copies:
        copy.start()
    for copy in copies:
        copy.wait()


def fetch(weight, after):
    return pl.pallas_call(
        fetch_kernel,
        in_specs=[pl.BlockSpec(memory_space=pl.ANY)] * 2,
        out_specs=[whole(), whole()],
        out_shape=[
            jax.ShapeDtypeStruct((WIDTH, GROUP), BF16),
            jax.ShapeDtypeStruct((2, WIDTH, GROUP), BF16),
        ],
        scratch_shapes=[pltpu.SemaphoreType.DMA((2,))],
        compiler_params=params(),
    )(weight, after)


def rope_tables():
    uly = lax.axis_index("uly")
    lane = np.arange(HD)
    section = np.where(lane < RT, 0, np.where(lane < RT + RH, 1, 2))
    start = np.array([0, RT, RT + RH])[section]
    length = np.array([RT, RH, RH])[section]
    half = length // 2
    upper = (lane - start) >= half
    index = jnp.asarray((lane - start) % half, F32)
    rates = 256.0 ** (-2.0 * index / jnp.asarray(length, F32))
    place = jnp.arange(TOKENS, dtype=jnp.int32)
    slot, dy, within = place // PAIR, place // LOCAL % 2, place % LOCAL
    ex = jnp.where(slot == 0, 0, (slot + 1) % 3 + 1)
    member = ((uly // 2) ^ ex) * 2 + ((uly % 2) ^ dy)
    frames_at = within // 16
    rows_at = lax.axis_index("blk") * 2 + within // 8 % 2
    columns_at = member * 8 + within % 8
    where = jnp.where(
        section[None, :] == 0,
        frames_at[:, None],
        jnp.where(section[None, :] == 1, rows_at[:, None], columns_at[:, None]),
    ).astype(F32)
    angles = where * rates[None, :]
    sign = jnp.asarray(np.where(upper, 1.0, -1.0), F32)
    return jnp.cos(angles), jnp.sin(angles) * sign[None, :]


def rope_partner(values):
    lane = lax.broadcasted_iota(jnp.int32, values.shape, 1)
    time_half, space_half = RT // 2, RH // 2
    first = jnp.where(
        lane < time_half,
        pltpu.roll(values, HD - time_half, axis=1),
        pltpu.roll(values, time_half, axis=1),
    )
    low = (lane < RT + space_half) | ((lane >= RT + RH) & (lane < RT + RH + space_half))
    rest = jnp.where(
        low, pltpu.roll(values, HD - space_half, axis=1), pltpu.roll(values, space_half, axis=1)
    )
    return jnp.where(lane < RT, first, rest)


def headed(mixed, gain, cosine, sine):
    out = []
    for head in range(HEADS):
        one = mixed[:, head * HD : (head + 1) * HD]
        one = one * lax.rsqrt(jnp.mean(one * one, axis=-1, keepdims=True) + 1e-06) * gain
        out.append((one * cosine + rope_partner(one) * sine).astype(BF16))
    return jnp.concatenate(out, axis=1)


def key_value_kernel(a0, a1, a2, a3, b0, b1, weight, gain, cosine, sine, out, gathered):
    for step, ref in enumerate((a0, a1, a2, a3)):
        gathered[step * PAIR : (step + 1) * PAIR, :LEFT] = ref[...]
        for side, other in enumerate((b0, b1)):
            start = step * PAIR + side * LOCAL
            gathered[start : start + LOCAL, LEFT:] = other[step * LOCAL : (step + 1) * LOCAL, :]
    keys = jnp.dot(gathered[...], weight[0], preferred_element_type=F32)
    out[0] = headed(keys, gain[...], cosine[...], sine[...])
    out[1] = jnp.dot(gathered[...], weight[1], preferred_element_type=F32).astype(BF16)


def project_key_value(pieces, weight, gain, cosine, sine):
    return pl.pallas_call(
        key_value_kernel,
        out_shape=[
            jax.ShapeDtypeStruct((2, TOKENS, GROUP), BF16),
            jax.ShapeDtypeStruct((TOKENS, WIDTH), BF16),
        ],
        compiler_params=params(),
    )(*pieces, weight, gain, cosine, sine)


def query_kernel(gathered, weight, gain, cosine, sine, out):
    mixed = jnp.dot(gathered[...], weight[...], preferred_element_type=F32)
    out[...] = headed(mixed, gain[...], cosine[...], sine[...])


def project_query(gathered, weight, gain, cosine, sine):
    return pl.pallas_call(
        query_kernel,
        out_shape=jax.ShapeDtypeStruct((TOKENS, GROUP), BF16),
        compiler_params=params(),
    )(gathered, weight, gain, cosine, sine)


def attend_items(items, blocks):
    scores = [
        [
            lax.dot_general(
                ref[0, :, lanes], query, (((1,), (1,)), ((), ())), preferred_element_type=F32
            )
            for ref in blocks
        ]
        for query, lanes, _ in items
    ]
    tops = [
        functools.reduce(jnp.maximum, [jnp.max(part, axis=0, keepdims=True) for part in score])
        for score in scores
    ]
    tops = [
        top if old is None else jnp.maximum(top, old[1]) for top, (_, _, old) in zip(tops, items)
    ]
    raised = [
        [jnp.exp2(part * SCALE2 - top * SCALE2) for part in score]
        for score, top in zip(scores, tops)
    ]
    results = []
    for part, top, (_, lanes, old) in zip(raised, tops, items):
        denominator = functools.reduce(
            jnp.add, [jnp.sum(one, axis=0, keepdims=True) for one in part]
        )
        numerator = functools.reduce(
            jnp.add,
            [
                lax.dot_general(
                    ref[1, :, lanes],
                    one.astype(BF16),
                    (((0,), (0,)), ((), ())),
                    preferred_element_type=F32,
                )
                for one, ref in zip(part, blocks)
            ],
        )
        if old is not None:
            fade = jnp.exp2((old[1] - top) * SCALE2)
            numerator = numerator + old[0] * fade
            denominator = denominator + old[2] * fade
        results.append((numerator, top, denominator))
    return results


def head_lanes(head):
    return slice(head * HD, (head + 1) * HD)


def old_state(total, stat, head):
    return (
        total[head_lanes(head), :],
        stat[head : head + 1, :],
        stat[HEADS + head : HEADS + head + 1, :],
    )


def attend_kernel(count, fresh, *refs):
    queries, blocks, refs = refs[0], refs[1 : 1 + count], refs[1 + count :]
    if not fresh:
        old_total, old_stat, refs = refs[0], refs[1], refs[2:]
    total, stat = refs
    items = [
        (
            queries[:, head_lanes(head)],
            head_lanes(head),
            None if fresh else old_state(old_total, old_stat, head),
        )
        for head in range(HEADS)
    ]
    for head, (numerator, top, denominator) in enumerate(attend_items(items, blocks)):
        total[head_lanes(head), :] = numerator
        stat[head : head + 1, :] = top
        stat[HEADS + head : HEADS + head + 1, :] = denominator


def attend(queries, blocks, state):
    count = queries.shape[0]
    return pl.pallas_call(
        functools.partial(attend_kernel, len(blocks), state is None),
        out_shape=[
            jax.ShapeDtypeStruct((GROUP, count), F32),
            jax.ShapeDtypeStruct((8, count), F32),
        ],
        compiler_params=params(),
    )(queries, *blocks, *(() if state is None else state))


def pack_levels(levels):
    rows = []
    for level in levels:
        for _ in range(3):
            coarse = level.astype(BF16).astype(F32)
            rows.append(coarse)
            level = level - coarse
    rows.append(jnp.zeros((STATS - len(rows),) + levels[0].shape[1:], F32))
    return jnp.concatenate(rows, axis=0).astype(BF16)


def finish_kernel(start, count, *refs):
    queries, blocks, refs = refs[0], refs[1 : 1 + count], refs[1 + count :]
    old_total, old_stat, out = refs
    at = slice(start, start + 2 * TOKENS)
    items = []
    for head in range(HEADS):
        lanes = head_lanes(head)
        old = (
            old_total[lanes, at],
            old_stat[head : head + 1, at],
            old_stat[HEADS + head : HEADS + head + 1, at],
        )
        items.append((queries[at, lanes], lanes, old))
    levels = []
    for head, (numerator, top, denominator) in enumerate(attend_items(items, blocks)):
        out[head_lanes(head), :] = (numerator / denominator).astype(BF16)
        levels.append(top * SCALE2 + jnp.log2(denominator))
    out[GROUP:, :] = pack_levels(levels)


def finish(queries, blocks, state, start):
    return pl.pallas_call(
        functools.partial(finish_kernel, start, len(blocks)),
        out_shape=jax.ShapeDtypeStruct((GROUP + STATS, 2 * TOKENS), BF16),
        compiler_params=params(),
    )(queries, *blocks, *state)


def merged(parts):
    tails = [part[GROUP:].astype(F32) for part in parts]
    outs, levels = [], []
    for head in range(HEADS):
        lanes = head_lanes(head)
        first = 3 * head
        level = [
            tail[first : first + 1] + tail[first + 1 : first + 2] + tail[first + 2 : first + 3]
            for tail in tails
        ]
        top = functools.reduce(jnp.maximum, level)
        shares = [jnp.exp2(one - top) for one in level]
        whole_share = functools.reduce(jnp.add, shares)
        mixed = functools.reduce(
            jnp.add, [part[lanes].astype(F32) * share for part, share in zip(parts, shares)]
        )
        outs.append((mixed / whole_share).astype(BF16))
        levels.append(top + jnp.log2(whole_share))
    return outs, levels


def merge_kernel(mine, theirs, *outs):
    heads, levels = merged([mine[...], theirs[...]])
    packed = pack_levels(levels)
    for index, out in enumerate(outs):
        lanes = slice(index * MINE, (index + 1) * MINE)
        for head in range(HEADS):
            out[head_lanes(head), :] = heads[head][:, lanes]
        out[GROUP:, :] = packed[:, lanes]


def merge(mine, theirs):
    return pl.pallas_call(
        merge_kernel,
        out_shape=[jax.ShapeDtypeStruct((GROUP + STATS, MINE), BF16)] * 4,
        compiler_params=params(),
    )(mine, theirs)


def out_kernel(mine, across, beside, beyond, weight, other_weight, keep, *sends):
    over = (((0,), (0,)), ((), ()))
    own = jnp.concatenate(merged([mine[...], across[...]])[0], axis=0)
    other = jnp.concatenate(merged([beside[...], beyond[...]])[0], axis=0)
    for start in range(0, WIDTH, HALF):
        lanes = slice(start, start + HALF)
        product = lax.dot_general(own, weight[:, lanes], over, preferred_element_type=F32)
        product += lax.dot_general(other, other_weight[:, lanes], over, preferred_element_type=F32)
        keep[:, lanes] = product[:LOCAL]
        for index, out in enumerate(sends):
            out[:, lanes] = product[(index + 1) * LOCAL : (index + 2) * LOCAL].astype(BF16)


def out_project(parts, weight, other_weight):
    return pl.pallas_call(
        out_kernel,
        out_shape=[jax.ShapeDtypeStruct((LOCAL, WIDTH), F32)]
        + [jax.ShapeDtypeStruct((LOCAL, WIDTH), BF16)] * 3,
        compiler_params=params(),
    )(*parts, weight, other_weight)


def final_kernel(
    tokens, keep, a, b, c, gate, shift, scale, weight, bias, block_out, latent
):
    wide = lambda ref: ref[...].astype(F32)
    projected = (keep[...] + wide(a)) + (wide(b) + wide(c))
    result = (wide(tokens) + gate[...] * projected).astype(BF16)
    block_out[...] = result
    final_in = (normed(result.astype(F32)) * (1.0 + scale[...]) + shift[...]).astype(BF16)
    mixed = jnp.dot(final_in, weight[...], preferred_element_type=F32)
    latent[...] = (mixed + bias[...]).astype(BF16)


def final(tokens, parts, gate, shift, scale, weight, bias):
    return pl.pallas_call(
        final_kernel,
        out_shape=[
            jax.ShapeDtypeStruct((LOCAL, WIDTH), BF16),
            jax.ShapeDtypeStruct((LOCAL, bias.shape[1]), BF16),
        ],
        compiler_params=params(),
    )(tokens, *parts, gate, shift, scale, weight, bias)


def halo(axis, first, end):
    place = lax.axis_index(axis)
    count = lax.axis_size(axis)
    odd = place % 2 == 1
    inner = lax.ppermute(jnp.where(odd, first, end), axis, [(i, i ^ 1) for i in range(count)])
    links = [(i, i + 1) for i in range(1, count - 1, 2)]
    outer = lax.ppermute(
        jnp.where(odd, end, first), axis, links + [(target, source) for source, target in links]
    )
    inner, outer = lax.optimization_barrier((inner, outer))
    low = jnp.where(place == 0, first, jnp.where(odd, inner, outer))
    high = jnp.where(place == count - 1, end, jnp.where(odd, outer, inner))
    return low, high


def local(
    block_in,
    mod_shift,
    mod_scale,
    mod_gate,
    qkv_weight,
    q_gain,
    k_gain,
    out_weight,
    final_shift,
    final_scale,
    final_weight,
    final_bias,
    conv_weight,
    conv_bias,
):
    frames, rows, columns, width = block_in.shape
    tokens = block_in.reshape(LOCAL, WIDTH)
    core = lax.axis_index("blk") % 2
    row = lambda vector: vector.reshape(1, -1)
    left, right = modulate(tokens, mod_scale, mod_shift)
    across_left = send_uly(left, ey=1)
    rights = [right] + spread_x(right)
    pair = jnp.concatenate([left, across_left], axis=0)
    quad = jnp.concatenate(rights, axis=0)
    lefts = [pair] + spread_x(pair)
    query_weight, key_value_weight = fetch(qkv_weight, across_left)
    pieces = lefts + [quad, send_uly(quad, ey=1)]
    cosine, sine = rope_tables()

    key_value, gathered = project_key_value(pieces, key_value_weight, row(k_gain), cosine, sine)
    half = lax.dynamic_slice_in_dim(out_weight, core * (GROUP // 2), GROUP // 2, 0)
    near_chain, half = lax.optimization_barrier((key_value, half))
    far_chain = send_blk(near_chain, dc=1)
    half = send_uly(half, ex=1)
    blocks = [send_ring(near_chain), send_ring(far_chain)]
    gathered, _ = lax.optimization_barrier((gathered, far_chain))
    query = project_query(gathered, query_weight, row(q_gain), cosine, sine)
    near = jnp.concatenate([query, send_blk(query, dy=1)], axis=0)
    queries = jnp.concatenate([near, send_blk(near, dc=1)], axis=0)

    state = attend(queries, [key_value] + blocks, None)
    blocks = [send_ring(block) for block in blocks]
    later, state = lax.optimization_barrier((blocks[1], state))
    state = attend(queries, [blocks[0], later], state)
    blocks = [send_ring(blocks[0]), send_ring(later)]
    last, state = lax.optimization_barrier((blocks[0], state))
    state = attend(queries, [last, blocks[1]], state)
    last = send_ring(last)

    theirs = finish(queries, [last], state, 2 * TOKENS)
    half, theirs = lax.optimization_barrier((half, theirs))
    mine = finish(queries, [last], state, 0)
    mine, beside, across, beyond = merge(mine, send_blk(theirs, dc=1))
    half, beside = lax.optimization_barrier((half, beside))
    other_half = send_blk(half, dc=1)
    other_weight = jnp.where(
        core == 0,
        jnp.concatenate([half, other_half], axis=0),
        jnp.concatenate([other_half, half], axis=0),
    )
    beyond = send_both(beyond, 1, 1)
    parts = [mine, send_blk(across, dy=1), send_uly(beside, ex=1), beyond]
    shares = out_project(parts, out_weight, other_weight)
    parts = [
        shares[0],
        send_uly(shares[3], ex=3, ey=1),
        send_uly(shares[2], ex=3),
        send_uly(shares[1], ey=1),
    ]
    block_out, latent_tok = final(
        tokens,
        parts,
        row(mod_gate),
        row(final_shift),
        row(final_scale),
        final_weight,
        row(final_bias),
    )

    channels = final_bias.shape[0] // 4
    latent = (
        latent_tok.reshape(frames, rows, columns, channels, 2, 2)
        .transpose(0, 1, 4, 2, 5, 3)
        .reshape(frames, 2 * rows, 2 * columns, channels)
    )
    above, below = halo("blk", latent[:, :1], latent[:, -1:])
    before, after = halo("uly", latent[:, :, :1], latent[:, :, -1:])
    above, below, before, after = lax.optimization_barrier((above, below, before, after))
    sides = jnp.concatenate([before, after], axis=2)
    above_sides, below_sides = halo("blk", sides[:, :1], sides[:, -1:])
    padded = jnp.concatenate(
        [
            jnp.concatenate([above_sides[:, :, :1], above, above_sides[:, :, 1:]], axis=2),
            jnp.concatenate([before, latent, after], axis=2),
            jnp.concatenate([below_sides[:, :, :1], below, below_sides[:, :, 1:]], axis=2),
        ],
        axis=1,
    )
    padded = jnp.concatenate([padded[:1], padded[:1], padded], axis=0)
    windows = []
    for time_lag in range(3):
        for row_lag in range(3):
            for column_lag in range(3):
                windows.append(
                    padded[
                        time_lag : time_lag + frames,
                        row_lag : row_lag + 2 * rows,
                        column_lag : column_lag + 2 * columns,
                    ]
                )
    patches = jnp.concatenate(windows, axis=-1)
    kernel = conv_weight.reshape(27 * channels, conv_weight.shape[-1])
    conv_out = (jnp.dot(patches, kernel, preferred_element_type=F32) + conv_bias).astype(BF16)
    return (block_out.reshape(frames, rows, columns, width), conv_out)


def solution(mesh):
    in_specs = (
        P(None, "blk", "uly", None),
        P(),
        P(),
        P(),
        P(None, None, "uly"),
        P(),
        P(),
        P("uly", None),
        P(),
        P(),
        P(),
        P(),
        P(),
        P(),
    )
    out_specs = (P(None, "blk", "uly", None), P(None, "blk", "uly", None))
    return jax.shard_map(local, mesh=mesh, in_specs=in_specs, out_specs=out_specs, check_vma=False)
```

```python
import functools

import jax
import jax.numpy as jnp
import numpy as np
from jax import lax
from jax.experimental import pallas as pl
from jax.experimental.pallas import tpu as pltpu
from jax.sharding import PartitionSpec as P

HD = 128
RT = 16
RH = 56
Z = 8
X = 4
HEADS = 3
GROUP = HEADS * HD
WIDTH = 3072
LOCAL = 32
PAIR = 2 * LOCAL
TOKENS = X * PAIR
STATS = 16
HALF = WIDTH // 2
LEFT = 1280
RIGHT = WIDTH - LEFT
MINE = TOKENS // 2
ORDER = (0, 3, 1, 2)
SCALE2 = float(HD ** (-0.5) / np.log(2.0))
F32 = jnp.float32
BF16 = jnp.bfloat16


def params(mib=12):
    return pltpu.CompilerParams(vmem_limit_bytes=mib * 1024 * 1024)


def whole():
    return pl.BlockSpec(memory_space=pltpu.VMEM)


def full(shape):
    return pl.BlockSpec(shape, lambda *_: (0,) * len(shape))


def blk_pairs(dy, dz, dc):
    return [
        (y * 2 * Z + z * 2 + c, (y ^ dy) * 2 * Z + (z + dz) % Z * 2 + (c ^ dc))
        for y in range(2)
        for z in range(Z)
        for c in range(2)
    ]


def ring_pairs():
    return [
        (y * 2 * Z + z * 2 + c, y * 2 * Z + (z + 1 - 2 * c) % Z * 2 + c)
        for y in range(2)
        for z in range(Z)
        for c in range(2)
    ]


def uly_pairs(ex, ey):
    return [(x * 2 + y, (x ^ ex) * 2 + (y ^ ey)) for x in range(X) for y in range(2)]


def send_blk(value, dy=0, dz=0, dc=0):
    return lax.ppermute(value, "blk", blk_pairs(dy, dz, dc))


def send_ring(value):
    return lax.ppermute(value, "blk", ring_pairs())


def send_uly(value, ex=0, ey=0):
    return lax.ppermute(value, "uly", uly_pairs(ex, ey))


def spread_x(value):
    came = {ex: send_uly(value, ex=ex) for ex in (2, 3, 1)}
    return [came[ex] for ex in ORDER[1:]]


def send_both(value, dy, ex):
    count = X * 2
    pairs = [
        (b * count + u, to_b * count + to_u)
        for b, to_b in blk_pairs(dy, 0, 0)
        for u, to_u in uly_pairs(ex, 0)
    ]
    return lax.ppermute(value, ("blk", "uly"), pairs)


def normed(values):
    center = values - jnp.mean(values, axis=-1, keepdims=True)
    spread = jnp.mean(center * center, axis=-1, keepdims=True)
    return center * lax.rsqrt(spread + 1e-06)


def modulate_kernel(tokens, scale_shift, left, right):
    scale, shift = scale_shift[0:1, :], scale_shift[1:2, :]
    x_mod = (normed(tokens[...].astype(F32)) * (1.0 + scale) + shift).astype(BF16)
    left[...] = x_mod[:, :LEFT]
    right[...] = x_mod[:, LEFT:]


def modulate(tokens, scale, shift):
    return pl.pallas_call(
        modulate_kernel,
        out_shape=[
            jax.ShapeDtypeStruct((LOCAL, LEFT), BF16),
            jax.ShapeDtypeStruct((LOCAL, RIGHT), BF16),
        ],
        compiler_params=params(),
    )(tokens, jnp.stack([scale, shift]))


def fetch_kernel(weight, after, query, key_value, sems):
    copies = [
        pltpu.make_async_copy(weight.at[0], query, sems.at[0]),
        pltpu.make_async_copy(weight.at[pl.ds(1, 2)], key_value, sems.at[1]),
    ]
    for copy in copies:
        copy.start()
    for copy in copies:
        copy.wait()


def fetch(weight, after):
    return pl.pallas_call(
        fetch_kernel,
        in_specs=[pl.BlockSpec(memory_space=pl.ANY)] * 2,
        out_specs=[whole(), whole()],
        out_shape=[
            jax.ShapeDtypeStruct((WIDTH, GROUP), BF16),
            jax.ShapeDtypeStruct((2, WIDTH, GROUP), BF16),
        ],
        scratch_shapes=[pltpu.SemaphoreType.DMA((2,))],
        compiler_params=params(),
    )(weight, after)


def rope_tables():
    uly = lax.axis_index("uly")
    lane = np.arange(HD)
    section = np.where(lane < RT, 0, np.where(lane < RT + RH, 1, 2))
    start = np.array([0, RT, RT + RH])[section]
    length = np.array([RT, RH, RH])[section]
    half = length // 2
    upper = (lane - start) >= half
    index = jnp.asarray((lane - start) % half, F32)
    rates = 256.0 ** (-2.0 * index / jnp.asarray(length, F32))
    place = jnp.arange(TOKENS, dtype=jnp.int32)
    slot, dy, within = place // PAIR, place // LOCAL % 2, place % LOCAL
    ex = jnp.where(slot == 0, 0, (slot + 1) % 3 + 1)
    member = ((uly // 2) ^ ex) * 2 + ((uly % 2) ^ dy)
    frames_at = within // 16
    rows_at = lax.axis_index("blk") * 2 + within // 8 % 2
    columns_at = member * 8 + within % 8
    where = jnp.where(
        section[None, :] == 0,
        frames_at[:, None],
        jnp.where(section[None, :] == 1, rows_at[:, None], columns_at[:, None]),
    ).astype(F32)
    angles = where * rates[None, :]
    sign = jnp.asarray(np.where(upper, 1.0, -1.0), F32)
    return jnp.cos(angles), jnp.sin(angles) * sign[None, :]


def rope_partner(values):
    lane = lax.broadcasted_iota(jnp.int32, values.shape, 1)
    time_half, space_half = RT // 2, RH // 2
    first = jnp.where(
        lane < time_half,
        pltpu.roll(values, HD - time_half, axis=1),
        pltpu.roll(values, time_half, axis=1),
    )
    low = (lane < RT + space_half) | ((lane >= RT + RH) & (lane < RT + RH + space_half))
    rest = jnp.where(
        low, pltpu.roll(values, HD - space_half, axis=1), pltpu.roll(values, space_half, axis=1)
    )
    return jnp.where(lane < RT, first, rest)


def headed(mixed, gain, cosine, sine):
    out = []
    for head in range(HEADS):
        one = mixed[:, head * HD : (head + 1) * HD]
        one = one * lax.rsqrt(jnp.mean(one * one, axis=-1, keepdims=True) + 1e-06) * gain
        out.append((one * cosine + rope_partner(one) * sine).astype(BF16))
    return jnp.concatenate(out, axis=1)


def key_value_kernel(a0, a1, a2, a3, b0, b1, weight, gain, cosine, sine, out, gathered):
    for step, ref in enumerate((a0, a1, a2, a3)):
        gathered[step * PAIR : (step + 1) * PAIR, :LEFT] = ref[...]
        for side, other in enumerate((b0, b1)):
            start = step * PAIR + side * LOCAL
            gathered[start : start + LOCAL, LEFT:] = other[step * LOCAL : (step + 1) * LOCAL, :]
    keys = jnp.dot(gathered[...], weight[0], preferred_element_type=F32)
    out[0] = headed(keys, gain[...], cosine[...], sine[...])
    out[1] = jnp.dot(gathered[...], weight[1], preferred_element_type=F32).astype(BF16)


def project_key_value(pieces, weight, gain, cosine, sine):
    return pl.pallas_call(
        key_value_kernel,
        out_shape=[
            jax.ShapeDtypeStruct((2, TOKENS, GROUP), BF16),
            jax.ShapeDtypeStruct((TOKENS, WIDTH), BF16),
        ],
        compiler_params=params(),
    )(*pieces, weight, gain, cosine, sine)


def query_kernel(gathered, weight, gain, cosine, sine, out):
    mixed = jnp.dot(gathered[...], weight[...], preferred_element_type=F32)
    out[...] = headed(mixed, gain[...], cosine[...], sine[...])


def project_query(gathered, weight, gain, cosine, sine):
    return pl.pallas_call(
        query_kernel,
        out_shape=jax.ShapeDtypeStruct((TOKENS, GROUP), BF16),
        compiler_params=params(),
    )(gathered, weight, gain, cosine, sine)


def attend_items(items, blocks):
    scores = [
        [
            lax.dot_general(
                ref[0, :, lanes], query, (((1,), (1,)), ((), ())), preferred_element_type=F32
            )
            for ref in blocks
        ]
        for query, lanes, _ in items
    ]
    tops = [
        functools.reduce(jnp.maximum, [jnp.max(part, axis=0, keepdims=True) for part in score])
        for score in scores
    ]
    tops = [
        top if old is None else jnp.maximum(top, old[1]) for top, (_, _, old) in zip(tops, items)
    ]
    raised = [
        [jnp.exp2(part * SCALE2 - top * SCALE2) for part in score]
        for score, top in zip(scores, tops)
    ]
    results = []
    for part, top, (_, lanes, old) in zip(raised, tops, items):
        denominator = functools.reduce(
            jnp.add, [jnp.sum(one, axis=0, keepdims=True) for one in part]
        )
        numerator = functools.reduce(
            jnp.add,
            [
                lax.dot_general(
                    ref[1, :, lanes],
                    one.astype(BF16),
                    (((0,), (0,)), ((), ())),
                    preferred_element_type=F32,
                )
                for one, ref in zip(part, blocks)
            ],
        )
        if old is not None:
            fade = jnp.exp2((old[1] - top) * SCALE2)
            numerator = numerator + old[0] * fade
            denominator = denominator + old[2] * fade
        results.append((numerator, top, denominator))
    return results


def head_lanes(head):
    return slice(head * HD, (head + 1) * HD)


def old_state(total, stat, head):
    return (
        total[head_lanes(head), :],
        stat[head : head + 1, :],
        stat[HEADS + head : HEADS + head + 1, :],
    )


def attend_kernel(count, fresh, *refs):
    queries, blocks, refs = refs[0], refs[1 : 1 + count], refs[1 + count :]
    if not fresh:
        old_total, old_stat, refs = refs[0], refs[1], refs[2:]
    total, stat = refs
    items = [
        (
            queries[:, head_lanes(head)],
            head_lanes(head),
            None if fresh else old_state(old_total, old_stat, head),
        )
        for head in range(HEADS)
    ]
    for head, (numerator, top, denominator) in enumerate(attend_items(items, blocks)):
        total[head_lanes(head), :] = numerator
        stat[head : head + 1, :] = top
        stat[HEADS + head : HEADS + head + 1, :] = denominator


def attend(queries, blocks, state):
    count = queries.shape[0]
    return pl.pallas_call(
        functools.partial(attend_kernel, len(blocks), state is None),
        out_shape=[
            jax.ShapeDtypeStruct((GROUP, count), F32),
            jax.ShapeDtypeStruct((8, count), F32),
        ],
        compiler_params=params(),
    )(queries, *blocks, *(() if state is None else state))


def pack_levels(levels):
    rows = []
    for level in levels:
        for _ in range(3):
            coarse = level.astype(BF16).astype(F32)
            rows.append(coarse)
            level = level - coarse
    rows.append(jnp.zeros((STATS - len(rows),) + levels[0].shape[1:], F32))
    return jnp.concatenate(rows, axis=0).astype(BF16)


def finish_kernel(start, count, *refs):
    queries, blocks, refs = refs[0], refs[1 : 1 + count], refs[1 + count :]
    old_total, old_stat, out = refs
    at = slice(start, start + 2 * TOKENS)
    items = []
    for head in range(HEADS):
        lanes = head_lanes(head)
        old = (
            old_total[lanes, at],
            old_stat[head : head + 1, at],
            old_stat[HEADS + head : HEADS + head + 1, at],
        )
        items.append((queries[at, lanes], lanes, old))
    levels = []
    for head, (numerator, top, denominator) in enumerate(attend_items(items, blocks)):
        out[head_lanes(head), :] = (numerator / denominator).astype(BF16)
        levels.append(top * SCALE2 + jnp.log2(denominator))
    out[GROUP:, :] = pack_levels(levels)


def finish(queries, blocks, state, start):
    return pl.pallas_call(
        functools.partial(finish_kernel, start, len(blocks)),
        out_shape=jax.ShapeDtypeStruct((GROUP + STATS, 2 * TOKENS), BF16),
        compiler_params=params(),
    )(queries, *blocks, *state)


def merged(parts):
    tails = [part[GROUP:].astype(F32) for part in parts]
    outs, levels = [], []
    for head in range(HEADS):
        lanes = head_lanes(head)
        first = 3 * head
        level = [
            tail[first : first + 1] + tail[first + 1 : first + 2] + tail[first + 2 : first + 3]
            for tail in tails
        ]
        top = functools.reduce(jnp.maximum, level)
        shares = [jnp.exp2(one - top) for one in level]
        whole_share = functools.reduce(jnp.add, shares)
        mixed = functools.reduce(
            jnp.add, [part[lanes].astype(F32) * share for part, share in zip(parts, shares)]
        )
        outs.append((mixed / whole_share).astype(BF16))
        levels.append(top + jnp.log2(whole_share))
    return outs, levels


def merge_kernel(mine, theirs, *outs):
    heads, levels = merged([mine[...], theirs[...]])
    packed = pack_levels(levels)
    for index, out in enumerate(outs):
        lanes = slice(index * MINE, (index + 1) * MINE)
        for head in range(HEADS):
            out[head_lanes(head), :] = heads[head][:, lanes]
        out[GROUP:, :] = packed[:, lanes]


def merge(mine, theirs):
    return pl.pallas_call(
        merge_kernel,
        out_shape=[jax.ShapeDtypeStruct((GROUP + STATS, MINE), BF16)] * 4,
        compiler_params=params(),
    )(mine, theirs)


def out_kernel(mine, across, beside, beyond, weight, other_weight, keep, *sends):
    over = (((0,), (0,)), ((), ()))
    own = jnp.concatenate(merged([mine[...], across[...]])[0], axis=0)
    other = jnp.concatenate(merged([beside[...], beyond[...]])[0], axis=0)
    for start in range(0, WIDTH, HALF):
        lanes = slice(start, start + HALF)
        product = lax.dot_general(own, weight[:, lanes], over, preferred_element_type=F32)
        product += lax.dot_general(other, other_weight[:, lanes], over, preferred_element_type=F32)
        keep[:, lanes] = product[:LOCAL]
        for index, out in enumerate(sends):
            out[:, lanes] = product[(index + 1) * LOCAL : (index + 2) * LOCAL].astype(BF16)


def out_project(parts, weight, other_weight):
    return pl.pallas_call(
        out_kernel,
        out_shape=[jax.ShapeDtypeStruct((LOCAL, WIDTH), F32)]
        + [jax.ShapeDtypeStruct((LOCAL, WIDTH), BF16)] * 3,
        compiler_params=params(),
    )(*parts, weight, other_weight)


def final_kernel(
    tokens, keep, a, b, c, gate, shift, scale, weight, bias, block_out, latent
):
    wide = lambda ref: ref[...].astype(F32)
    projected = (keep[...] + wide(a)) + (wide(b) + wide(c))
    result = (wide(tokens) + gate[...] * projected).astype(BF16)
    block_out[...] = result
    final_in = (normed(result.astype(F32)) * (1.0 + scale[...]) + shift[...]).astype(BF16)
    mixed = jnp.dot(final_in, weight[...], preferred_element_type=F32)
    latent[...] = (mixed + bias[...]).astype(BF16)


def final(tokens, parts, gate, shift, scale, weight, bias):
    return pl.pallas_call(
        final_kernel,
        out_shape=[
            jax.ShapeDtypeStruct((LOCAL, WIDTH), BF16),
            jax.ShapeDtypeStruct((LOCAL, bias.shape[1]), BF16),
        ],
        compiler_params=params(),
    )(tokens, *parts, gate, shift, scale, weight, bias)


def halo(axis, first, end):
    place = lax.axis_index(axis)
    count = lax.axis_size(axis)
    odd = place % 2 == 1
    inner = lax.ppermute(jnp.where(odd, first, end), axis, [(i, i ^ 1) for i in range(count)])
    links = [(i, i + 1) for i in range(1, count - 1, 2)]
    outer = lax.ppermute(
        jnp.where(odd, end, first), axis, links + [(target, source) for source, target in links]
    )
    inner, outer = lax.optimization_barrier((inner, outer))
    low = jnp.where(place == 0, first, jnp.where(odd, inner, outer))
    high = jnp.where(place == count - 1, end, jnp.where(odd, outer, inner))
    return low, high


def local(
    block_in,
    mod_shift,
    mod_scale,
    mod_gate,
    qkv_weight,
    q_gain,
    k_gain,
    out_weight,
    final_shift,
    final_scale,
    final_weight,
    final_bias,
    conv_weight,
    conv_bias,
):
    frames, rows, columns, width = block_in.shape
    tokens = block_in.reshape(LOCAL, WIDTH)
    core = lax.axis_index("blk") % 2
    row = lambda vector: vector.reshape(1, -1)
    left, right = modulate(tokens, mod_scale, mod_shift)
    across_left = send_uly(left, ey=1)
    rights = [right] + spread_x(right)
    pair = jnp.concatenate([left, across_left], axis=0)
    quad = jnp.concatenate(rights, axis=0)
    lefts = [pair] + spread_x(pair)
    query_weight, key_value_weight = fetch(qkv_weight, across_left)
    pieces = lefts + [quad, send_uly(quad, ey=1)]
    cosine, sine = rope_tables()

    key_value, gathered = project_key_value(pieces, key_value_weight, row(k_gain), cosine, sine)
    half = lax.dynamic_slice_in_dim(out_weight, core * (GROUP // 2), GROUP // 2, 0)
    near_chain, half = lax.optimization_barrier((key_value, half))
    far_chain = send_blk(near_chain, dc=1)
    half = send_uly(half, ex=1)
    blocks = [send_ring(near_chain), send_ring(far_chain)]
    gathered, _ = lax.optimization_barrier((gathered, far_chain))
    query = project_query(gathered, query_weight, row(q_gain), cosine, sine)
    near = jnp.concatenate([query, send_blk(query, dy=1)], axis=0)
    queries = jnp.concatenate([near, send_blk(near, dc=1)], axis=0)

    state = attend(queries, [key_value] + blocks, None)
    blocks = [send_ring(block) for block in blocks]
    later, state = lax.optimization_barrier((blocks[1], state))
    state = attend(queries, [blocks[0], later], state)
    blocks = [send_ring(blocks[0]), send_ring(later)]
    last, state = lax.optimization_barrier((blocks[0], state))
    state = attend(queries, [last, blocks[1]], state)
    last = send_ring(last)

    theirs = finish(queries, [last], state, 2 * TOKENS)
    half, theirs = lax.optimization_barrier((half, theirs))
    mine = finish(queries, [last], state, 0)
    mine, beside, across, beyond = merge(mine, send_blk(theirs, dc=1))
    half, beside = lax.optimization_barrier((half, beside))
    other_half = send_blk(half, dc=1)
    other_weight = jnp.where(
        core == 0,
        jnp.concatenate([half, other_half], axis=0),
        jnp.concatenate([other_half, half], axis=0),
    )
    beyond = send_both(beyond, 1, 1)
    parts = [mine, send_blk(across, dy=1), send_uly(beside, ex=1), beyond]
    shares = out_project(parts, out_weight, other_weight)
    parts = [
        shares[0],
        send_uly(shares[3], ex=3, ey=1),
        send_uly(shares[2], ex=3),
        send_uly(shares[1], ey=1),
    ]
    block_out, latent_tok = final(
        tokens,
        parts,
        row(mod_gate),
        row(final_shift),
        row(final_scale),
        final_weight,
        row(final_bias),
    )

    channels = final_bias.shape[0] // 4
    latent = (
        latent_tok.reshape(frames, rows, columns, channels, 2, 2)
        .transpose(0, 1, 4, 2, 5, 3)
        .reshape(frames, 2 * rows, 2 * columns, channels)
    )
    low, high = halo("blk", latent[:, :1], latent[:, -1:])
    padded = jnp.concatenate([low, latent, high], axis=1)
    low, high = halo("uly", padded[:, :, :1], padded[:, :, -1:])
    padded = jnp.concatenate([low, padded, high], axis=2)
    padded = jnp.concatenate([padded[:1], padded[:1], padded], axis=0)
    windows = []
    for time_lag in range(3):
        for row_lag in range(3):
            for column_lag in range(3):
                windows.append(
                    padded[
                        time_lag : time_lag + frames,
                        row_lag : row_lag + 2 * rows,
                        column_lag : column_lag + 2 * columns,
                    ]
                )
    patches = jnp.concatenate(windows, axis=-1)
    kernel = conv_weight.reshape(27 * channels, conv_weight.shape[-1])
    conv_out = (jnp.dot(patches, kernel, preferred_element_type=F32) + conv_bias).astype(BF16)
    return (block_out.reshape(frames, rows, columns, width), conv_out)


def solution(mesh):
    in_specs = (
        P(None, "blk", "uly", None),
        P(),
        P(),
        P(),
        P(None, None, "uly"),
        P(),
        P(),
        P("uly", None),
        P(),
        P(),
        P(),
        P(),
        P(),
        P(),
    )
    out_specs = (P(None, "blk", "uly", None), P(None, "blk", "uly", None))
    return jax.shard_map(local, mesh=mesh, in_specs=in_specs, out_specs=out_specs, check_vma=False)
```

```python
import functools

import jax
import jax.numpy as jnp
import numpy as np
from jax import lax
from jax.experimental import pallas as pl
from jax.experimental.pallas import tpu as pltpu
from jax.sharding import PartitionSpec as P

HD = 128
RT = 16
RH = 56
Z = 8
X = 4
HEADS = 3
GROUP = HEADS * HD
WIDTH = 3072
LOCAL = 32
PAIR = 2 * LOCAL
TOKENS = X * PAIR
STATS = 16
HALF = WIDTH // 2
LEFT = 1280
RIGHT = WIDTH - LEFT
MINE = TOKENS // 2
ORDER = (0, 3, 1, 2)
SCALE2 = float(HD ** (-0.5) / np.log(2.0))
F32 = jnp.float32
BF16 = jnp.bfloat16


def params(mib=12):
    return pltpu.CompilerParams(vmem_limit_bytes=mib * 1024 * 1024)


def whole():
    return pl.BlockSpec(memory_space=pltpu.VMEM)


def full(shape):
    return pl.BlockSpec(shape, lambda *_: (0,) * len(shape))


def blk_pairs(dy, dz, dc):
    return [
        (y * 2 * Z + z * 2 + c, (y ^ dy) * 2 * Z + (z + dz) % Z * 2 + (c ^ dc))
        for y in range(2)
        for z in range(Z)
        for c in range(2)
    ]


def ring_pairs():
    return [
        (y * 2 * Z + z * 2 + c, y * 2 * Z + (z + 1 - 2 * c) % Z * 2 + c)
        for y in range(2)
        for z in range(Z)
        for c in range(2)
    ]


def uly_pairs(ex, ey):
    return [(x * 2 + y, (x ^ ex) * 2 + (y ^ ey)) for x in range(X) for y in range(2)]


def send_blk(value, dy=0, dz=0, dc=0):
    return lax.ppermute(value, "blk", blk_pairs(dy, dz, dc))


def send_ring(value):
    return lax.ppermute(value, "blk", ring_pairs())


def send_uly(value, ex=0, ey=0):
    return lax.ppermute(value, "uly", uly_pairs(ex, ey))


def spread_x(value):
    came = {ex: send_uly(value, ex=ex) for ex in (2, 3, 1)}
    return [came[ex] for ex in ORDER[1:]]


def send_both(value, dy, ex):
    count = X * 2
    pairs = [
        (b * count + u, to_b * count + to_u)
        for b, to_b in blk_pairs(dy, 0, 0)
        for u, to_u in uly_pairs(ex, 0)
    ]
    return lax.ppermute(value, ("blk", "uly"), pairs)


def normed(values):
    center = values - jnp.mean(values, axis=-1, keepdims=True)
    spread = jnp.mean(center * center, axis=-1, keepdims=True)
    return center * lax.rsqrt(spread + 1e-06)


def modulate_kernel(tokens, scale_shift, left, right):
    scale, shift = scale_shift[0:1, :], scale_shift[1:2, :]
    x_mod = (normed(tokens[...].astype(F32)) * (1.0 + scale) + shift).astype(BF16)
    left[...] = x_mod[:, :LEFT]
    right[...] = x_mod[:, LEFT:]


def modulate(tokens, scale, shift):
    return pl.pallas_call(
        modulate_kernel,
        out_shape=[
            jax.ShapeDtypeStruct((LOCAL, LEFT), BF16),
            jax.ShapeDtypeStruct((LOCAL, RIGHT), BF16),
        ],
        compiler_params=params(),
    )(tokens, jnp.stack([scale, shift]))


def fetch_kernel(weight, after, query, key_value, sems):
    copies = [
        pltpu.make_async_copy(weight.at[0], query, sems.at[0]),
        pltpu.make_async_copy(weight.at[pl.ds(1, 2)], key_value, sems.at[1]),
    ]
    for copy in copies:
        copy.start()
    for copy in copies:
        copy.wait()


def fetch(weight, after):
    return pl.pallas_call(
        fetch_kernel,
        in_specs=[pl.BlockSpec(memory_space=pl.ANY)] * 2,
        out_specs=[whole(), whole()],
        out_shape=[
            jax.ShapeDtypeStruct((WIDTH, GROUP), BF16),
            jax.ShapeDtypeStruct((2, WIDTH, GROUP), BF16),
        ],
        scratch_shapes=[pltpu.SemaphoreType.DMA((2,))],
        compiler_params=params(),
    )(weight, after)


def rope_tables():
    uly = lax.axis_index("uly")
    lane = np.arange(HD)
    section = np.where(lane < RT, 0, np.where(lane < RT + RH, 1, 2))
    start = np.array([0, RT, RT + RH])[section]
    length = np.array([RT, RH, RH])[section]
    half = length // 2
    upper = (lane - start) >= half
    index = jnp.asarray((lane - start) % half, F32)
    rates = 256.0 ** (-2.0 * index / jnp.asarray(length, F32))
    place = jnp.arange(TOKENS, dtype=jnp.int32)
    slot, dy, within = place // PAIR, place // LOCAL % 2, place % LOCAL
    ex = jnp.where(slot == 0, 0, (slot + 1) % 3 + 1)
    member = ((uly // 2) ^ ex) * 2 + ((uly % 2) ^ dy)
    frames_at = within // 16
    rows_at = lax.axis_index("blk") * 2 + within // 8 % 2
    columns_at = member * 8 + within % 8
    where = jnp.where(
        section[None, :] == 0,
        frames_at[:, None],
        jnp.where(section[None, :] == 1, rows_at[:, None], columns_at[:, None]),
    ).astype(F32)
    angles = where * rates[None, :]
    sign = jnp.asarray(np.where(upper, 1.0, -1.0), F32)
    return jnp.cos(angles), jnp.sin(angles) * sign[None, :]


def rope_partner(values):
    lane = lax.broadcasted_iota(jnp.int32, values.shape, 1)
    time_half, space_half = RT // 2, RH // 2
    first = jnp.where(
        lane < time_half,
        pltpu.roll(values, HD - time_half, axis=1),
        pltpu.roll(values, time_half, axis=1),
    )
    low = (lane < RT + space_half) | ((lane >= RT + RH) & (lane < RT + RH + space_half))
    rest = jnp.where(
        low, pltpu.roll(values, HD - space_half, axis=1), pltpu.roll(values, space_half, axis=1)
    )
    return jnp.where(lane < RT, first, rest)


def headed(mixed, gain, cosine, sine):
    out = []
    for head in range(HEADS):
        one = mixed[:, head * HD : (head + 1) * HD]
        one = one * lax.rsqrt(jnp.mean(one * one, axis=-1, keepdims=True) + 1e-06) * gain
        out.append((one * cosine + rope_partner(one) * sine).astype(BF16))
    return jnp.concatenate(out, axis=1)


def key_value_kernel(a0, a1, a2, a3, b0, b1, weight, gain, cosine, sine, out, gathered):
    for step, ref in enumerate((a0, a1, a2, a3)):
        gathered[step * PAIR : (step + 1) * PAIR, :LEFT] = ref[...]
        for side, other in enumerate((b0, b1)):
            start = step * PAIR + side * LOCAL
            gathered[start : start + LOCAL, LEFT:] = other[step * LOCAL : (step + 1) * LOCAL, :]
    keys = jnp.dot(gathered[...], weight[0], preferred_element_type=F32)
    out[0] = headed(keys, gain[...], cosine[...], sine[...])
    out[1] = jnp.dot(gathered[...], weight[1], preferred_element_type=F32).astype(BF16)


def project_key_value(pieces, weight, gain, cosine, sine):
    return pl.pallas_call(
        key_value_kernel,
        out_shape=[
            jax.ShapeDtypeStruct((2, TOKENS, GROUP), BF16),
            jax.ShapeDtypeStruct((TOKENS, WIDTH), BF16),
        ],
        compiler_params=params(),
    )(*pieces, weight, gain, cosine, sine)


def query_kernel(gathered, weight, gain, cosine, sine, out):
    mixed = jnp.dot(gathered[...], weight[...], preferred_element_type=F32)
    out[...] = headed(mixed, gain[...], cosine[...], sine[...])


def project_query(gathered, weight, gain, cosine, sine):
    return pl.pallas_call(
        query_kernel,
        out_shape=jax.ShapeDtypeStruct((TOKENS, GROUP), BF16),
        compiler_params=params(),
    )(gathered, weight, gain, cosine, sine)


def attend_items(items, blocks):
    scores = [
        [
            lax.dot_general(
                ref[0, :, lanes], query, (((1,), (1,)), ((), ())), preferred_element_type=F32
            )
            for ref in blocks
        ]
        for query, lanes, _ in items
    ]
    tops = [
        functools.reduce(jnp.maximum, [jnp.max(part, axis=0, keepdims=True) for part in score])
        for score in scores
    ]
    tops = [
        top if old is None else jnp.maximum(top, old[1]) for top, (_, _, old) in zip(tops, items)
    ]
    raised = [
        [jnp.exp2(part * SCALE2 - top * SCALE2) for part in score]
        for score, top in zip(scores, tops)
    ]
    results = []
    for part, top, (_, lanes, old) in zip(raised, tops, items):
        denominator = functools.reduce(
            jnp.add, [jnp.sum(one, axis=0, keepdims=True) for one in part]
        )
        numerator = functools.reduce(
            jnp.add,
            [
                lax.dot_general(
                    ref[1, :, lanes],
                    one.astype(BF16),
                    (((0,), (0,)), ((), ())),
                    preferred_element_type=F32,
                )
                for one, ref in zip(part, blocks)
            ],
        )
        if old is not None:
            fade = jnp.exp2((old[1] - top) * SCALE2)
            numerator = numerator + old[0] * fade
            denominator = denominator + old[2] * fade
        results.append((numerator, top, denominator))
    return results


def head_lanes(head):
    return slice(head * HD, (head + 1) * HD)


def old_state(total, stat, head):
    return (
        total[head_lanes(head), :],
        stat[head : head + 1, :],
        stat[HEADS + head : HEADS + head + 1, :],
    )


def attend_kernel(count, fresh, *refs):
    queries, blocks, refs = refs[0], refs[1 : 1 + count], refs[1 + count :]
    if not fresh:
        old_total, old_stat, refs = refs[0], refs[1], refs[2:]
    total, stat = refs
    items = [
        (
            queries[:, head_lanes(head)],
            head_lanes(head),
            None if fresh else old_state(old_total, old_stat, head),
        )
        for head in range(HEADS)
    ]
    for head, (numerator, top, denominator) in enumerate(attend_items(items, blocks)):
        total[head_lanes(head), :] = numerator
        stat[head : head + 1, :] = top
        stat[HEADS + head : HEADS + head + 1, :] = denominator


def attend(queries, blocks, state):
    count = queries.shape[0]
    return pl.pallas_call(
        functools.partial(attend_kernel, len(blocks), state is None),
        out_shape=[
            jax.ShapeDtypeStruct((GROUP, count), F32),
            jax.ShapeDtypeStruct((8, count), F32),
        ],
        compiler_params=params(),
    )(queries, *blocks, *(() if state is None else state))


def pack_levels(levels):
    rows = []
    for level in levels:
        for _ in range(3):
            coarse = level.astype(BF16).astype(F32)
            rows.append(coarse)
            level = level - coarse
    rows.append(jnp.zeros((STATS - len(rows),) + levels[0].shape[1:], F32))
    return jnp.concatenate(rows, axis=0).astype(BF16)


def finish_kernel(start, count, *refs):
    queries, blocks, refs = refs[0], refs[1 : 1 + count], refs[1 + count :]
    old_total, old_stat, out = refs
    at = slice(start, start + 2 * TOKENS)
    items = []
    for head in range(HEADS):
        lanes = head_lanes(head)
        old = (
            old_total[lanes, at],
            old_stat[head : head + 1, at],
            old_stat[HEADS + head : HEADS + head + 1, at],
        )
        items.append((queries[at, lanes], lanes, old))
    levels = []
    for head, (numerator, top, denominator) in enumerate(attend_items(items, blocks)):
        out[head_lanes(head), :] = (numerator / denominator).astype(BF16)
        levels.append(top * SCALE2 + jnp.log2(denominator))
    out[GROUP:, :] = pack_levels(levels)


def finish(queries, blocks, state, start):
    return pl.pallas_call(
        functools.partial(finish_kernel, start, len(blocks)),
        out_shape=jax.ShapeDtypeStruct((GROUP + STATS, 2 * TOKENS), BF16),
        compiler_params=params(),
    )(queries, *blocks, *state)


def merged(parts):
    tails = [part[GROUP:].astype(F32) for part in parts]
    outs, levels = [], []
    for head in range(HEADS):
        lanes = head_lanes(head)
        first = 3 * head
        level = [
            tail[first : first + 1] + tail[first + 1 : first + 2] + tail[first + 2 : first + 3]
            for tail in tails
        ]
        top = functools.reduce(jnp.maximum, level)
        shares = [jnp.exp2(one - top) for one in level]
        whole_share = functools.reduce(jnp.add, shares)
        mixed = functools.reduce(
            jnp.add, [part[lanes].astype(F32) * share for part, share in zip(parts, shares)]
        )
        outs.append((mixed / whole_share).astype(BF16))
        levels.append(top + jnp.log2(whole_share))
    return outs, levels


def merge_kernel(mine, theirs, *outs):
    heads, levels = merged([mine[...], theirs[...]])
    packed = pack_levels(levels)
    for index, out in enumerate(outs):
        lanes = slice(index * MINE, (index + 1) * MINE)
        for head in range(HEADS):
            out[head_lanes(head), :] = heads[head][:, lanes]
        out[GROUP:, :] = packed[:, lanes]


def merge(mine, theirs):
    return pl.pallas_call(
        merge_kernel,
        out_shape=[jax.ShapeDtypeStruct((GROUP + STATS, MINE), BF16)] * 4,
        compiler_params=params(),
    )(mine, theirs)


def out_kernel(mine, across, beside, beyond, weight, other_weight, keep, *sends):
    over = (((0,), (0,)), ((), ()))
    own = jnp.concatenate(merged([mine[...], across[...]])[0], axis=0)
    other = jnp.concatenate(merged([beside[...], beyond[...]])[0], axis=0)
    for start in range(0, WIDTH, HALF):
        lanes = slice(start, start + HALF)
        product = lax.dot_general(own, weight[:, lanes], over, preferred_element_type=F32)
        product += lax.dot_general(other, other_weight[:, lanes], over, preferred_element_type=F32)
        keep[:, lanes] = product[:LOCAL]
        for index, out in enumerate(sends):
            out[:, lanes] = product[(index + 1) * LOCAL : (index + 2) * LOCAL].astype(BF16)


def out_project(parts, weight, other_weight):
    return pl.pallas_call(
        out_kernel,
        out_shape=[jax.ShapeDtypeStruct((LOCAL, WIDTH), F32)]
        + [jax.ShapeDtypeStruct((LOCAL, WIDTH), BF16)] * 3,
        compiler_params=params(),
    )(*parts, weight, other_weight)


def final_kernel(
    tokens, keep, a, b, c, gate, shift, scale, weight, bias, block_out, latent
):
    wide = lambda ref: ref[...].astype(F32)
    projected = (keep[...] + wide(a)) + (wide(b) + wide(c))
    result = (wide(tokens) + gate[...] * projected).astype(BF16)
    block_out[...] = result
    final_in = (normed(result.astype(F32)) * (1.0 + scale[...]) + shift[...]).astype(BF16)
    mixed = jnp.dot(final_in, weight[...], preferred_element_type=F32)
    latent[...] = (mixed + bias[...]).astype(BF16)


def final(tokens, parts, gate, shift, scale, weight, bias):
    return pl.pallas_call(
        final_kernel,
        out_shape=[
            jax.ShapeDtypeStruct((LOCAL, WIDTH), BF16),
            jax.ShapeDtypeStruct((LOCAL, bias.shape[1]), BF16),
        ],
        compiler_params=params(),
    )(tokens, *parts, gate, shift, scale, weight, bias)


def halo(axis, first, end):
    place = lax.axis_index(axis)
    count = lax.axis_size(axis)
    odd = place % 2 == 1
    inner = lax.ppermute(jnp.where(odd, first, end), axis, [(i, i ^ 1) for i in range(count)])
    links = [(i, i + 1) for i in range(1, count - 1, 2)]
    outer = lax.ppermute(
        jnp.where(odd, end, first), axis, links + [(target, source) for source, target in links]
    )
    inner, outer = lax.optimization_barrier((inner, outer))
    low = jnp.where(place == 0, first, jnp.where(odd, inner, outer))
    high = jnp.where(place == count - 1, end, jnp.where(odd, outer, inner))
    return low, high


def local(
    block_in,
    mod_shift,
    mod_scale,
    mod_gate,
    qkv_weight,
    q_gain,
    k_gain,
    out_weight,
    final_shift,
    final_scale,
    final_weight,
    final_bias,
    conv_weight,
    conv_bias,
):
    frames, rows, columns, width = block_in.shape
    tokens = block_in.reshape(LOCAL, WIDTH)
    core = lax.axis_index("blk") % 2
    row = lambda vector: vector.reshape(1, -1)
    left, right = modulate(tokens, mod_scale, mod_shift)
    across_left = send_uly(left, ey=1)
    rights = [right] + spread_x(right)
    pair = jnp.concatenate([left, across_left], axis=0)
    quad = jnp.concatenate(rights, axis=0)
    lefts = [pair] + spread_x(pair)
    query_weight, key_value_weight = fetch(qkv_weight, across_left)
    pieces = lefts + [quad, send_uly(quad, ey=1)]
    cosine, sine = rope_tables()

    key_value, gathered = project_key_value(pieces, key_value_weight, row(k_gain), cosine, sine)
    half = lax.dynamic_slice_in_dim(out_weight, core * (GROUP // 2), GROUP // 2, 0)
    near_chain, half = lax.optimization_barrier((key_value, half))
    far_chain = send_blk(near_chain, dc=1)
    half = send_uly(half, ex=1)
    blocks = [send_ring(near_chain), send_ring(far_chain)]
    gathered, _ = lax.optimization_barrier((gathered, far_chain))
    query = project_query(gathered, query_weight, row(q_gain), cosine, sine)
    near = jnp.concatenate([query, send_blk(query, dy=1)], axis=0)
    queries = jnp.concatenate([near, send_blk(near, dc=1)], axis=0)

    state = attend(queries, [key_value] + blocks, None)
    blocks = [send_ring(block) for block in blocks]
    second = blocks
    third = [send_ring(block) for block in second]
    last, state = lax.optimization_barrier((third[0], state))
    state = attend(queries, second, state)
    state = attend(queries, [last, third[1]], state)
    last = send_ring(last)

    theirs = finish(queries, [last], state, 2 * TOKENS)
    half, theirs = lax.optimization_barrier((half, theirs))
    mine = finish(queries, [last], state, 0)
    mine, beside, across, beyond = merge(mine, send_blk(theirs, dc=1))
    half, beside = lax.optimization_barrier((half, beside))
    other_half = send_blk(half, dc=1)
    other_weight = jnp.where(
        core == 0,
        jnp.concatenate([half, other_half], axis=0),
        jnp.concatenate([other_half, half], axis=0),
    )
    beyond = send_both(beyond, 1, 1)
    parts = [mine, send_blk(across, dy=1), send_uly(beside, ex=1), beyond]
    shares = out_project(parts, out_weight, other_weight)
    parts = [
        shares[0],
        send_uly(shares[3], ex=3, ey=1),
        send_uly(shares[2], ex=3),
        send_uly(shares[1], ey=1),
    ]
    block_out, latent_tok = final(
        tokens,
        parts,
        row(mod_gate),
        row(final_shift),
        row(final_scale),
        final_weight,
        row(final_bias),
    )

    channels = final_bias.shape[0] // 4
    latent = (
        latent_tok.reshape(frames, rows, columns, channels, 2, 2)
        .transpose(0, 1, 4, 2, 5, 3)
        .reshape(frames, 2 * rows, 2 * columns, channels)
    )
    low, high = halo("blk", latent[:, :1], latent[:, -1:])
    padded = jnp.concatenate([low, latent, high], axis=1)
    low, high = halo("uly", padded[:, :, :1], padded[:, :, -1:])
    padded = jnp.concatenate([low, padded, high], axis=2)
    padded = jnp.concatenate([padded[:1], padded[:1], padded], axis=0)
    windows = []
    for time_lag in range(3):
        for row_lag in range(3):
            for column_lag in range(3):
                windows.append(
                    padded[
                        time_lag : time_lag + frames,
                        row_lag : row_lag + 2 * rows,
                        column_lag : column_lag + 2 * columns,
                    ]
                )
    patches = jnp.concatenate(windows, axis=-1)
    kernel = conv_weight.reshape(27 * channels, conv_weight.shape[-1])
    conv_out = (jnp.dot(patches, kernel, preferred_element_type=F32) + conv_bias).astype(BF16)
    return (block_out.reshape(frames, rows, columns, width), conv_out)


def solution(mesh):
    in_specs = (
        P(None, "blk", "uly", None),
        P(),
        P(),
        P(),
        P(None, None, "uly"),
        P(),
        P(),
        P("uly", None),
        P(),
        P(),
        P(),
        P(),
        P(),
        P(),
    )
    out_specs = (P(None, "blk", "uly", None), P(None, "blk", "uly", None))
    return jax.shard_map(local, mesh=mesh, in_specs=in_specs, out_specs=out_specs, check_vma=False)
```
